256 devices in a mesh: ctx: 64 (over z, y, core), head: 4 (over x).
Axes of the slice: x: 4, y: 4, z: 8, core: 2. Of those that a mesh axis runs over, the one named last changes fastest.
Arguments:
- queries: bfloat16 [32768, 2048], P('ctx', 'head'), may hold values from -8 to 8
- keys: bfloat16 [32768, 512], P('ctx', 'head'), may hold values from -12 to 12
- values: bfloat16 [32768, 512], P('ctx', 'head'), may hold values from -6 to 6
- picks: int32 [64, 4, 7], P(None, 'head'), may hold values from 0 to 62, as said below
- out_weight: bfloat16 [2048, 4096], P('head'), may hold values from -0.125 to 0.125
Outputs:
- projected: bfloat16 [32768, 4096], P(('ctx', 'head'))
The draws below stay inside these ranges and needn't reach their ends.
Inputs may be any that keep to these rules, and one draw needn't show every extreme that they name: `picks`: for query block b and KV head h the first entry is max(b - 1, 0) and every entry lies in 0 to max(b - 1, 0); entries of one list may repeat.
All inputs are finite; a program needn't handle non-finite values.
Results may differ from the reference program's by a relative error of at most 0.018.
Values may be sent and summed in bfloat16 or wider, within the bound.
No kernel may reach another device: no remote copies, remote signals or barrier semaphores. Data moves between devices by JAX's collectives and lax.ppermute only.
A program may use at most 128 MiB of HBM per device.

```python
import jax
import jax.numpy as jnp
from jax import lax

HD = 128
KVH = 4
QPK = 4
D = 4096
BLOCK = 512
TOPK = 8
QH = 16
TOKENS = 32768


def draw_queries(key, part):
    key = jax.random.fold_in(key, 1)
    block_count = TOKENS // BLOCK
    shape = (block_count, BLOCK, KVH, QPK, HD)
    base = jnp.clip(jax.random.normal(key, shape, jnp.float32), -6.0, 6.0)
    return jnp.clip(base, -8.0, 8.0).reshape(TOKENS, KVH * QPK * HD).astype(jnp.bfloat16)


def draw_keys(key, part):
    key = jax.random.fold_in(key, 2)
    block_count = TOKENS // BLOCK
    noise_key, common_key = jax.random.split(key)
    shape = (block_count, BLOCK, KVH, HD)
    noise = 1.5 * jnp.clip(jax.random.normal(noise_key, shape, jnp.float32), -5.0, 5.0)
    common = 1.5 * jnp.clip(jax.random.normal(common_key, (block_count, 1, KVH, HD), jnp.float32), -3.0, 3.0)
    base = noise + common
    return jnp.clip(base, -12.0, 12.0).reshape(TOKENS, KVH * HD).astype(jnp.bfloat16)


def draw_values(key, part):
    key = jax.random.fold_in(key, 3)
    block_count = TOKENS // BLOCK
    noise_key, common_key = jax.random.split(key)
    shape = (block_count, BLOCK, KVH, HD)
    noise = jnp.clip(jax.random.normal(noise_key, shape, jnp.float32), -4.0, 4.0)
    common = 0.8 * jnp.clip(jax.random.normal(common_key, (block_count, 1, KVH, HD), jnp.float32), -2.5, 2.5)
    return jnp.clip(noise + common, -6.0, 6.0).reshape(TOKENS, KVH * HD).astype(jnp.bfloat16)


def draw_picks(key, part):
    key = jax.random.fold_in(key, 4)
    block_count = TOKENS // BLOCK
    raw = jax.random.randint(key, (block_count, KVH, TOPK - 1), 0, 1 << 20)
    limit = jnp.maximum(jnp.arange(block_count), 1)[:, None, None]
    chosen = raw % limit
    previous = jnp.maximum(jnp.arange(block_count) - 1, 0)[:, None, None]
    first = (jnp.arange(TOPK - 1) == 0)[None, None, :]
    return jnp.where(first, previous, chosen).astype(jnp.int32)


def level_of(key, shape, shards, least, largest):
    level, own = 1.0, jax.random.fold_in(key, 6)
    for dim, shards_of in shards:
        steps = jnp.exp(jax.random.uniform(jax.random.fold_in(own, dim), (shards_of,), jnp.float32, least / len(shards), largest / len(shards)))
        level = level * jnp.repeat(steps, shape[dim] // shards_of).reshape([-1 if axis == dim else 1 for axis in range(len(shape))])
    return level


def scatter_about(key, dims, spread, reach, pieces=(), kind=jnp.bfloat16):
    loudness = level_of(key, dims, pieces, -0.22, 0.18) if pieces else 1.0
    values = jax.random.normal(key, dims, jnp.float32) * spread * loudness
    return jnp.minimum(jnp.maximum(values, -reach), reach).astype(kind)


def setup_inputs(seed: int = 0) -> dict:
    splits = jax.random.split(jax.random.key(seed), 6)
    queries = draw_queries(jax.random.fold_in(splits[5], 71), 0)
    keys = draw_keys(jax.random.fold_in(splits[5], 71), 0)
    values = draw_values(jax.random.fold_in(splits[5], 71), 0)
    picks = draw_picks(jax.random.fold_in(splits[5], 71), 0)
    out_weight = scatter_about(splits[4], (QH * HD, D), (QH * HD) ** -0.5, 0.125, ((0, 4),))
    return dict(queries=queries, keys=keys, values=values, picks=picks, out_weight=out_weight)


def usable_picks(chosen, block_number):
    pick_count = chosen.shape[-1]
    matching = chosen[..., :, None] == chosen[..., None, :]
    earlier_pick = jnp.arange(pick_count)[:, None] > jnp.arange(pick_count)[None, :]
    repeated = jnp.any(matching & earlier_pick, axis=-1)
    return (chosen != block_number) & jnp.logical_not(repeated)


def attend_block(query, own_key, own_value, picked_key, picked_value, usable, mean_key, mean_value, earlier):
    highest = lax.Precision.HIGHEST
    length = query.shape[0]
    scaling = query.shape[-1] ** -0.5
    causal = jnp.arange(length)[:, None] >= jnp.arange(length)[None, :]

    def one_head(head_number):
        query_head = lax.dynamic_index_in_dim(query, head_number, 2, keepdims=False)
        own_scores = jnp.einsum("qhd,khd->hqk", query_head, own_key, precision=highest, preferred_element_type=jnp.float32) * scaling
        own_scores = jnp.where(causal[None], own_scores, -1e30)
        far_scores = jnp.einsum("qhd,hjkd->hqjk", query_head, picked_key, precision=highest, preferred_element_type=jnp.float32) * scaling
        far_scores = jnp.where(usable[:, None, :, None], far_scores, -1e30)
        row_top = jnp.maximum(jnp.max(own_scores, axis=2), jnp.max(far_scores, axis=(2, 3)))
        own_weights = jnp.exp(own_scores - row_top[:, :, None])
        far_weights = jnp.exp(far_scores - row_top[:, :, None, None])
        sparse_total = jnp.sum(own_weights, axis=2) + jnp.sum(far_weights, axis=(2, 3))
        own_rounded = own_weights.astype(jnp.bfloat16).astype(own_value.dtype)
        far_rounded = far_weights.astype(jnp.bfloat16).astype(own_value.dtype)
        gathered = jnp.einsum("hqk,khd->qhd", own_rounded, own_value, precision=highest, preferred_element_type=jnp.float32)
        gathered = gathered + jnp.einsum("hqjk,hjkd->qhd", far_rounded, picked_value, precision=highest, preferred_element_type=jnp.float32)
        sparse_out = gathered / jnp.transpose(sparse_total)[:, :, None]
        summary_scores = jnp.einsum("qhd,chd->hqc", query_head, mean_key, precision=highest, preferred_element_type=jnp.float32) * scaling
        summary_scores = jnp.where(earlier[None, None, :], summary_scores, -1e30)
        summary_top = jnp.maximum(jnp.max(summary_scores, axis=2), 0.0)
        summary_weights = jnp.exp(summary_scores - summary_top[:, :, None])
        summary_total = jnp.sum(summary_weights, axis=2) + jnp.exp(-summary_top)
        summary_rounded = summary_weights.astype(jnp.bfloat16).astype(mean_value.dtype)
        summary_out = jnp.einsum("hqc,chd->qhd", summary_rounded, mean_value, precision=highest, preferred_element_type=jnp.float32)
        summary_out = summary_out / jnp.transpose(summary_total)[:, :, None]
        return sparse_out + summary_out

    results = lax.map(one_head, jnp.arange(query.shape[2]))
    return jnp.transpose(results, (1, 2, 0, 3)).astype(jnp.bfloat16)


def reference(queries, keys, values, picks, out_weight):
    block_count = TOKENS // BLOCK
    query_blocks = queries.reshape(block_count, BLOCK, KVH, QPK, HD)
    key_blocks = keys.reshape(block_count, BLOCK, KVH, HD)
    value_blocks = values.reshape(block_count, BLOCK, KVH, HD)
    mean_key = jnp.mean(key_blocks, axis=1, dtype=jnp.float32).astype(jnp.bfloat16)
    mean_value = jnp.mean(value_blocks, axis=1, dtype=jnp.float32).astype(jnp.bfloat16)
    head_index = jnp.arange(KVH)[:, None]

    def per_block(block_number):
        chosen = picks[block_number]
        usable = usable_picks(chosen, block_number)
        picked_key = key_blocks[chosen, :, head_index, :].astype(jnp.float32)
        picked_value = value_blocks[chosen, :, head_index, :].astype(jnp.float32)
        earlier = jnp.arange(block_count) < block_number
        result = attend_block(query_blocks[block_number].astype(jnp.float32), key_blocks[block_number].astype(jnp.float32),
                              value_blocks[block_number].astype(jnp.float32), picked_key, picked_value, usable,
                              mean_key.astype(jnp.float32), mean_value.astype(jnp.float32), earlier)
        return result.reshape(BLOCK, KVH * QPK * HD)

    attended = lax.map(per_block, jnp.arange(block_count)).reshape(TOKENS, KVH * QPK * HD)
    return jnp.dot(attended, out_weight, preferred_element_type=jnp.float32).astype(jnp.bfloat16)
```

```python
import functools
import math

import jax
import jax.numpy as jnp
from jax import lax
from jax.experimental import pallas as pl
from jax.experimental.pallas import tpu as pltpu
from jax.sharding import Mesh
from jax.sharding import PartitionSpec as P

HD = 128
BLOCK = 512
QPK = 4
PICKS = 6
PIECES = 8
ROWS = BLOCK // PIECES
PART = PICKS * ROWS
MEAN_ROWS = 16
MSG = ROWS + MEAN_ROWS
HALF = PIECES // 2 * ROWS
NZ, NY, NC, NX = 8, 4, 2, 4
TILE = BLOCK // NX
STACK = TILE * QPK
SCALE = HD**-0.5 * math.log2(math.e)
FAR = 1e30
MIB = 1 << 20

VMEM = functools.partial(pl.BlockSpec, memory_space=pltpu.VMEM)
ANY = pl.BlockSpec(memory_space=pl.ANY)


def params(mib):
    return pltpu.CompilerParams(vmem_limit_bytes=mib * MIB)


def cost(flops, nbytes, trans=0):
    return pl.CostEstimate(flops=flops, bytes_accessed=nbytes, transcendentals=trans)


def pack_kernel(k_ref, v_ref, kv_ref, msg_ref):
    k = k_ref[...]
    v = v_ref[...]
    kv_ref[:, :HD] = k
    kv_ref[:, HD:] = v
    mk = jnp.sum(k.astype(jnp.float32), axis=0, keepdims=True) * (1.0 / BLOCK)
    mv = jnp.sum(v.astype(jnp.float32), axis=0, keepdims=True) * (1.0 / BLOCK)
    mean = jnp.concatenate([mk, mv], axis=1).astype(jnp.bfloat16)
    mean = jnp.broadcast_to(mean, (MEAN_ROWS, 2 * HD))
    for r in range(PIECES):
        rows = slice(r * ROWS, (r + 1) * ROWS)
        msg_ref[r, :ROWS, :HD] = k_ref[rows, :]
        msg_ref[r, :ROWS, HD:] = v_ref[rows, :]
        msg_ref[r, ROWS:, :] = mean


def pack(k, v):
    return pl.pallas_call(
        pack_kernel,
        out_shape=[
            jax.ShapeDtypeStruct((BLOCK, 2 * HD), jnp.bfloat16),
            jax.ShapeDtypeStruct((PIECES, MSG, 2 * HD), jnp.bfloat16),
        ],
        compiler_params=params(16),
        cost_estimate=cost(1 << 18, MIB),
        name="pack",
    )(k, v)


def unpack_kernel(msg_ref, a_ref, b_ref):
    row = lax.broadcasted_iota(jnp.int32, (MEAN_ROWS, 2 * HD), 0)
    for h, out in enumerate((a_ref, b_ref)):
        means = jnp.zeros((MEAN_ROWS, 2 * HD), jnp.float32)
        for i in range(PIECES // 2):
            s = h * (PIECES // 2) + i
            out[i * ROWS : (i + 1) * ROWS, :] = msg_ref[s, :ROWS, :]
            means = jnp.where(row == i, msg_ref[s, ROWS:, :].astype(jnp.float32), means)
        out[HALF:, :] = means.astype(jnp.bfloat16)


def unpack(msg):
    return pl.pallas_call(
        unpack_kernel,
        out_shape=[jax.ShapeDtypeStruct((HALF + MEAN_ROWS, 2 * HD), jnp.bfloat16)] * 2,
        compiler_params=params(16),
        cost_estimate=cost(1 << 18, MIB),
        name="unpack",
    )(msg)


def choose(refs, index, act):
    if len(refs) == 1:
        act(refs[0])
        return
    half = len(refs) // 2
    pl.when(index < half)(lambda: choose(refs[:half], index, act))
    pl.when(index >= half)(lambda: choose(refs[half:], index - half, act))


def pick_kernel(steps, place_ref, picks_ref, *refs):
    bufs, outs, sem = refs[: 2 * NZ], refs[2 * NZ + 1 : -1], refs[-1]
    z, y = place_ref[0], place_ref[1]
    for dy, out in zip(steps, outs):
        for dc in range(NC):
            dst = ((y + dy) & (NY - 1)) * NC + dc

            def step(j, carry, dst=dst, out=out, dc=dc):
                p = picks_ref[dst, j + 1]
                d = (z - lax.shift_right_logical(p, 3)) & (NZ - 1)
                h = lax.shift_right_logical(p, 2) & 1
                start = pl.multiple_of((p & 3) * ROWS, ROWS)
                to = pl.multiple_of((dc * PICKS + j) * ROWS, ROWS)

                def act(buf):
                    pltpu.make_async_copy(
                        buf.at[pl.ds(start, ROWS), :], out.at[pl.ds(to, ROWS), :], sem
                    ).start()

                choose(bufs, d * 2 + h, act)
                return carry

            lax.fori_loop(0, PICKS, step, 0)
    for out in outs:
        pltpu.make_async_copy(out, out, sem).wait()


def pick_pieces(steps, place, picks, bufs, after):
    return pl.pallas_call(
        functools.partial(pick_kernel, steps),
        grid_spec=pltpu.PrefetchScalarGridSpec(
            num_scalar_prefetch=2,
            grid=(1,),
            in_specs=[ANY] * (2 * NZ + 1),
            out_specs=[ANY] * len(steps),
            scratch_shapes=[pltpu.SemaphoreType.DMA(())],
        ),
        out_shape=[jax.ShapeDtypeStruct((NC * PART, 2 * HD), jnp.bfloat16)] * len(steps),
        compiler_params=params(16),
        cost_estimate=cost(0, MIB),
        name="pick_pieces",
    )(place, picks, *bufs, after)


def contract(a, b):
    return lax.dot_general(a, b, (((1,), (1,)), ((), ())), preferred_element_type=jnp.float32)


def stack_heads(q_ref, t):
    rows = slice(t * TILE, (t + 1) * TILE)
    return jnp.concatenate([q_ref[rows, g * HD : (g + 1) * HD] for g in range(QPK)], axis=0)


def row_max(xs, scale):
    top = jnp.max(xs[0], axis=1, keepdims=True)
    for x in xs[1:]:
        top = jnp.maximum(top, jnp.max(x, axis=1, keepdims=True))
    return top * scale


def save_state(out_ref, rows, acc, top):
    lane = lax.broadcasted_iota(jnp.int32, (STACK, HD), 1)
    out_ref[rows, :HD] = acc[:, :HD]
    out_ref[rows, HD:] = jnp.where(lane < HD // 2, acc[:, HD:], top)


def near_kernel(place_ref, q_ref, k_ref, v_ref, kv_ref, out_ref, own_v, prev_v):
    ones = jnp.ones((BLOCK, HD), jnp.bfloat16)
    own_v[:, :HD] = v_ref[...]
    own_v[:, HD:] = ones
    prev_v[:, :HD] = kv_ref[:, HD:]
    prev_v[:, HD:] = ones
    pen = jnp.where(place_ref[4] == 0, FAR, 0.0)
    for t in range(NX):
        q = stack_heads(q_ref, t)
        seen = (t + 1) * TILE
        token = lax.rem(lax.broadcasted_iota(jnp.int32, (STACK, seen), 0), TILE) + t * TILE
        key = lax.broadcasted_iota(jnp.int32, (STACK, seen), 1)
        own = jnp.where(key <= token, contract(q, k_ref[:seen, :]) * SCALE, -FAR)
        prev = contract(q, kv_ref[:, :HD]) * SCALE
        top = jnp.maximum(row_max([own], 1.0), row_max([prev], 1.0) - pen)
        own = jnp.exp2(own - top).astype(jnp.bfloat16)
        prev = jnp.exp2(prev - (top + pen)).astype(jnp.bfloat16)
        acc = jnp.dot(own, own_v[:seen, :], preferred_element_type=jnp.float32)
        acc += jnp.dot(prev, prev_v[...], preferred_element_type=jnp.float32)
        save_state(out_ref, slice(t * STACK, (t + 1) * STACK), acc, top)


def near_attention(place, q, k, v, kv):
    return pl.pallas_call(
        near_kernel,
        grid_spec=pltpu.PrefetchScalarGridSpec(
            num_scalar_prefetch=1,
            grid=(1,),
            in_specs=[
                pl.BlockSpec((BLOCK, QPK * HD), lambda i, place: (0, 0)),
                pl.BlockSpec((BLOCK, HD), lambda i, place: (0, 0)),
                pl.BlockSpec((BLOCK, HD), lambda i, place: (0, 0)),
                pl.BlockSpec((BLOCK, 2 * HD), lambda i, place: (0, 0)),
            ],
            out_specs=pl.BlockSpec((NX * STACK, 2 * HD), lambda i, place: (0, 0)),
            scratch_shapes=[pltpu.VMEM((BLOCK, 2 * HD), jnp.bfloat16)] * 2,
        ),
        out_shape=jax.ShapeDtypeStruct((NX * STACK, 2 * HD), jnp.float32),
        compiler_params=params(32),
        cost_estimate=cost(1 << 20, MIB),
        name="near_attention",
    )(place, q, k, v, kv)


def far_body(place_ref, picks_ref, q_ref, state_ref, pieces, v_all, finish):
    block = place_ref[4]
    own = block & (PIECES - 1)
    for j in range(1, PICKS + 1):
        p = picks_ref[own, j]
        bad = p == block
        for e in range(j):
            bad = bad | (p == picks_ref[own, e])
        keep = jnp.where(bad, 0.0, 1.0)
        ones = jnp.full((ROWS, HD), keep, jnp.float32).astype(jnp.bfloat16)
        for s, piece in enumerate(pieces):
            at = slice(s * PART + (j - 1) * ROWS, s * PART + j * ROWS)
            v = piece[(j - 1) * ROWS : j * ROWS, HD:]
            v_all[at, :HD] = (v.astype(jnp.float32) * keep).astype(jnp.bfloat16)
            v_all[at, HD:] = ones

    def scores(t):
        q = stack_heads(q_ref, t)
        return [contract(q, piece[:, :HD]) for piece in pieces]

    after = scores(0)
    for t in range(q_ref.shape[0] // TILE):
        xs = after
        if (t + 1) * TILE < q_ref.shape[0]:
            after = scores(t + 1)
        rows = slice(t * STACK, (t + 1) * STACK)
        state = state_ref[rows, :]
        top0 = state[:, 2 * HD - 1 :]
        top = jnp.maximum(top0, row_max(xs, SCALE))
        acc = None
        for s, x in enumerate(xs):
            w = jnp.exp2(x * SCALE - top).astype(jnp.bfloat16)
            part = jnp.dot(
                w, v_all[s * PART : (s + 1) * PART, :], preferred_element_type=jnp.float32
            )
            acc = part if acc is None else acc + part
        acc = state * jnp.exp2(top0 - top) + acc
        finish(t, rows, state, acc, top)


def far_kernel(count, place_ref, picks_ref, q_ref, state_ref, *refs):
    pieces, (out_ref, v_all) = refs[:count], refs[count:]

    def finish(t, rows, state, acc, top):
        save_state(out_ref, rows, acc, top)

    @pl.when(place_ref[4] == 0)
    def _():
        out_ref[...] = state_ref[...]

    @pl.when(place_ref[4] > 0)
    def _():
        far_body(place_ref, picks_ref, q_ref, state_ref, pieces, v_all, finish)


def far_specs(place_at, count):
    core = lambda i, place, picks: (place[2], 0)
    return [
        pl.BlockSpec((BLOCK, QPK * HD), lambda i, place, picks: (0, 0)),
        pl.BlockSpec((NX * STACK, 2 * HD), lambda i, place, picks: (0, 0)),
    ] + [pl.BlockSpec((PART, 2 * HD), core)] * count


def far_attention(place, picks, q, state, pieces):
    count = len(pieces)
    return pl.pallas_call(
        functools.partial(far_kernel, count),
        grid_spec=pltpu.PrefetchScalarGridSpec(
            num_scalar_prefetch=2,
            grid=(1,),
            in_specs=far_specs(2, count),
            out_specs=pl.BlockSpec((NX * STACK, 2 * HD), lambda i, place, picks: (0, 0)),
            scratch_shapes=[pltpu.VMEM((count * PART, 2 * HD), jnp.bfloat16)],
        ),
        out_shape=jax.ShapeDtypeStruct((NX * STACK, 2 * HD), jnp.float32),
        compiler_params=params(40),
        cost_estimate=cost(1 << 20, MIB),
        name="far_attention",
    )(place, picks, q, state, *pieces)


def last_kernel(count, place_ref, picks_ref, q_ref, state_ref, *refs):
    pieces = refs[:count]
    means = refs[count : count + 2 * NZ]
    out_ref, v_all, mean_k, mean_v = refs[count + 2 * NZ :]
    z, block = place_ref[0], place_ref[4]
    for s, mean in enumerate(means):
        rows = slice(s * MEAN_ROWS, (s + 1) * MEAN_ROWS)
        mean_k[rows, :] = mean[:, :HD]
        mean_v[rows, :HD] = mean[:, HD:]
    mean_v[:, HD:] = jnp.ones((2 * NZ * MEAN_ROWS, HD), jnp.bfloat16)

    s = lax.broadcasted_iota(jnp.int32, (1, 2 * NZ * MEAN_ROWS), 1)
    i4 = s & (MEAN_ROWS - 1)
    half = lax.shift_right_logical(s, 4) & 1
    zs = (z - lax.shift_right_logical(s, 5)) & (NZ - 1)
    number = zs * PIECES + half * (PIECES // 2) + i4
    bias = jnp.where((i4 < PIECES // 2) & (number < block), 0.0, -FAR)

    def finish(t, rows, state, acc, top):
        sparse = acc[:, :HD] / acc[:, HD : HD + 1]
        sums = contract(stack_heads(q_ref, t), mean_k[...]) * SCALE + bias
        high = jnp.maximum(jnp.max(sums, axis=1, keepdims=True), 0.0)
        w = jnp.exp2(sums - high).astype(jnp.bfloat16)
        summary = jnp.dot(w, mean_v[...], preferred_element_type=jnp.float32)
        total = summary[:, HD : HD + 1] + jnp.exp2(-high)
        result = (sparse + summary[:, :HD] / total).astype(jnp.bfloat16)
        for g in range(QPK):
            out_ref[t * TILE : (t + 1) * TILE, g * HD : (g + 1) * HD] = result[
                g * TILE : (g + 1) * TILE
            ]

    @pl.when(block == 0)
    def _():
        for t in range(NX):
            rows = slice(t * STACK, (t + 1) * STACK)
            finish(t, rows, state_ref[rows, :], state_ref[rows, :], None)

    @pl.when(block > 0)
    def _():
        far_body(place_ref, picks_ref, q_ref, state_ref, pieces, v_all, finish)


def last_attention(place, picks, q, state, pieces, bufs):
    count = len(pieces)
    mean_spec = pl.BlockSpec((MEAN_ROWS, 2 * HD), lambda i, place, picks: (HALF // MEAN_ROWS, 0))
    mean_count = 2 * NZ * MEAN_ROWS
    return pl.pallas_call(
        functools.partial(last_kernel, count),
        grid_spec=pltpu.PrefetchScalarGridSpec(
            num_scalar_prefetch=2,
            grid=(1,),
            in_specs=far_specs(2, count) + [mean_spec] * (2 * NZ),
            out_specs=pl.BlockSpec((BLOCK, QPK * HD), lambda i, place, picks: (0, 0)),
            scratch_shapes=[
                pltpu.VMEM((count * PART, 2 * HD), jnp.bfloat16),
                pltpu.VMEM((mean_count, HD), jnp.bfloat16),
                pltpu.VMEM((mean_count, 2 * HD), jnp.bfloat16),
            ],
        ),
        out_shape=jax.ShapeDtypeStruct((BLOCK, QPK * HD), jnp.bfloat16),
        compiler_params=params(40),
        cost_estimate=cost(1 << 20, MIB),
        name="last_attention",
    )(place, picks, q, state, *pieces, *bufs)


def project_kernel(place_ref, att_ref, w0, *refs):
    out_ref = refs[-1]
    r1, l1, r2, l2, r1s, l1s, r2s, l2s = refs[:-1]
    x, c = place_ref[3], place_ref[2]
    quarter = QPK * HD // 4
    mine = c * 2 * quarter
    other = 2 * quarter - mine

    def part(by, start, w):
        at = pl.multiple_of(((x + by) & (NX - 1)) * QPK * HD + start, quarter)
        a = att_ref[:, pl.ds(at, w.shape[0])]
        return jnp.dot(a, w[...], preferred_element_type=jnp.float32)

    acc = part(0, 0, w0)
    acc += part(-1, mine, r1) + part(-1, other, r1s)
    acc += part(1, mine, l1) + part(1, other, l1s)
    acc += part(2, mine, r2) + part(2, mine + quarter, l2)
    acc += part(2, other, r2s) + part(2, other + quarter, l2s)
    out_ref[...] = acc.astype(jnp.bfloat16)


def project(place, attended, w0, parts):
    width = w0.shape[1]
    tile = 512
    return pl.pallas_call(
        project_kernel,
        grid_spec=pltpu.PrefetchScalarGridSpec(
            num_scalar_prefetch=1,
            grid=(width // tile,),
            in_specs=[pl.BlockSpec((TILE, NX * QPK * HD), lambda n, place: (0, 0))]
            + [pl.BlockSpec((p.shape[0], tile), lambda n, place: (0, n)) for p in (w0, *parts)],
            out_specs=pl.BlockSpec((TILE, tile), lambda n, place: (0, n)),
        ),
        out_shape=jax.ShapeDtypeStruct((TILE, width), jnp.bfloat16),
        compiler_params=params(40),
        cost_estimate=cost(1 << 20, MIB),
        name="project",
    )(place, attended, w0, *parts)


def shift(x, axis, size, by):
    return lax.ppermute(x, axis, [(i, (i + by) % size) for i in range(size)])


def swap(x):
    return lax.ppermute(x, "c", [(0, 1), (1, 0)])


def gather_weight(w, c):
    rows = QPK * HD // 2
    half = lax.dynamic_slice_in_dim(w, c * rows, rows, 0)
    r1, l1 = shift(half, "x", NX, 1), shift(half, "x", NX, -1)
    r2 = shift(r1[: rows // 2], "x", NX, 1)
    l2 = shift(l1[rows // 2 :], "x", NX, -1)
    mine = [r1, l1, r2, l2]
    return mine + [swap(m) for m in mine]


def per_device(q, k, v, picks, w):
    z, y, c, x = (lax.axis_index(a).astype(jnp.int32) for a in ("z", "y", "c", "x"))
    place = jnp.stack([z, y, c, x, z * PIECES + y * NC + c])
    plane_picks = lax.dynamic_slice_in_dim(picks.reshape(picks.shape[0], -1), z * PIECES, PIECES, 0)

    weights = gather_weight(w, c)
    kv, msg = pack(k, v)
    msg = lax.all_to_all(msg, ("y", "c"), 0, 0, tiled=True)
    blocks = NZ * PIECES
    prev = lax.ppermute(kv, ("z", "y", "c"), [(i, i + 1) for i in range(blocks - 1)])
    a, b = unpack(msg)

    up, down = [(a, b)], [(a, b)]
    for d in range(3):
        up.append(tuple(shift(h, "z", NZ, 1) for h in up[-1]))
        down.append(tuple(shift(h, "z", NZ, -1) for h in down[-1]))
    far = (shift(up[3][0], "z", NZ, 1), shift(down[3][1], "z", NZ, -1))
    rings = up + [far] + [down[3], down[2], down[1]]
    bufs = [h for pair in rings for h in pair]
    state = near_attention(place, q, k, v, prev)

    here, right, left = pick_pieces((0, 1, NY - 1), place, plane_picks, bufs, state)
    right, left = shift(right, "y", NY, 1), shift(left, "y", NY, -1)
    state = far_attention(place, plane_picks, q, state, [here, swap(here)])
    (across,) = pick_pieces((2,), place, plane_picks, bufs, state)
    across = shift(across, "y", NY, 2)
    state = far_attention(
        place, plane_picks, q, state, [right, swap(right), left, swap(left)]
    )
    attended = last_attention(place, plane_picks, q, state, [across, swap(across)], bufs)

    rows = lax.all_to_all(attended.reshape(NX, TILE, QPK * HD), "x", 0, 0, tiled=True)
    rows = jnp.transpose(rows, (1, 0, 2)).reshape(TILE, NX * QPK * HD)
    return project(place, rows, w, weights)


def solution(mesh):
    fine = Mesh(mesh.devices.reshape(NZ, NY, NC, NX), ("z", "y", "c", "x"))
    ctx = ("z", "y", "c")
    in_specs = (P(ctx, "x"), P(ctx, "x"), P(ctx, "x"), P(None, "x", None), P("x", None))
    out_specs = P(("z", "y", "c", "x"), None)
    return jax.shard_map(
        per_device, mesh=fine, in_specs=in_specs, out_specs=out_specs, check_vma=False
    )
```

```python
import functools
import math

import jax
import jax.numpy as jnp
from jax import lax
from jax.experimental import pallas as pl
from jax.experimental.pallas import tpu as pltpu
from jax.sharding import Mesh
from jax.sharding import PartitionSpec as P

HD = 128
BLOCK = 512
QPK = 4
PICKS = 6
PIECES = 8
ROWS = BLOCK // PIECES
PART = PICKS * ROWS
MEAN_ROWS = 16
MSG = ROWS + MEAN_ROWS
HALF = PIECES // 2 * ROWS
NZ, NY, NC, NX = 8, 4, 2, 4
TILE = BLOCK // NX
STACK = TILE * QPK
SCALE = HD**-0.5 * math.log2(math.e)
WHALF = QPK * HD // NC
FAR = 1e30
MIB = 1 << 20

ANY = pl.BlockSpec(memory_space=pl.ANY)


def params(mib=40):
    return pltpu.CompilerParams(vmem_limit_bytes=mib * MIB)


def cost(flops, nbytes, trans=0):
    return pl.CostEstimate(flops=flops, bytes_accessed=nbytes, transcendentals=trans)


def pack_kernel(k_ref, v_ref, kv_ref, msg_ref):
    k = k_ref[...]
    v = v_ref[...]
    kv_ref[:, :HD] = k
    kv_ref[:, HD:] = v
    mk = jnp.sum(k.astype(jnp.float32), axis=0, keepdims=True) * (1.0 / BLOCK)
    mv = jnp.sum(v.astype(jnp.float32), axis=0, keepdims=True) * (1.0 / BLOCK)
    mean = jnp.concatenate([mk, mv], axis=1).astype(jnp.bfloat16)
    mean = jnp.broadcast_to(mean, (MEAN_ROWS, 2 * HD))
    for r in range(PIECES):
        rows = slice(r * ROWS, (r + 1) * ROWS)
        msg_ref[r, :ROWS, :HD] = k_ref[rows, :]
        msg_ref[r, :ROWS, HD:] = v_ref[rows, :]
        msg_ref[r, ROWS:, :] = mean


def pack(k, v):
    return pl.pallas_call(
        pack_kernel,
        out_shape=[
            jax.ShapeDtypeStruct((BLOCK, 2 * HD), jnp.bfloat16),
            jax.ShapeDtypeStruct((PIECES, MSG, 2 * HD), jnp.bfloat16),
        ],
        compiler_params=params(16),
        cost_estimate=cost(1 << 18, MIB),
        name="pack",
    )(k, v)


def unpack_kernel(msg_ref, a_ref, b_ref):
    row = lax.broadcasted_iota(jnp.int32, (MEAN_ROWS, 2 * HD), 0)
    for h, out in enumerate((a_ref, b_ref)):
        means = jnp.zeros((MEAN_ROWS, 2 * HD), jnp.float32)
        for i in range(PIECES // 2):
            s = h * (PIECES // 2) + i
            out[i * ROWS : (i + 1) * ROWS, :] = msg_ref[s, :ROWS, :]
            means = jnp.where(row == i, msg_ref[s, ROWS:, :].astype(jnp.float32), means)
        out[HALF:, :] = means.astype(jnp.bfloat16)


def unpack(msg):
    return pl.pallas_call(
        unpack_kernel,
        out_shape=[jax.ShapeDtypeStruct((HALF + MEAN_ROWS, 2 * HD), jnp.bfloat16)] * 2,
        compiler_params=params(16),
        cost_estimate=cost(1 << 18, MIB),
        name="unpack",
    )(msg)


def choose(refs, index, act):
    if len(refs) == 1:
        act(refs[0])
        return
    half = len(refs) // 2
    pl.when(index < half)(lambda: choose(refs[:half], index, act))
    pl.when(index >= half)(lambda: choose(refs[half:], index - half, act))


def pick_kernel(place_ref, picks_ref, *refs):
    bufs, below, above = refs[: 2 * NZ], refs[2 * NZ + 1], refs[2 * NZ + 2]
    out, low, high, sem, side_sem = refs[-5:]
    rows = WHALF // 2
    sides = [
        pltpu.make_async_copy(below.at[:rows, :], low, side_sem.at[0]),
        pltpu.make_async_copy(above.at[rows:, :], high, side_sem.at[1]),
    ]

    def step(n, carry):
        p = picks_ref[lax.div(n, PICKS), 1 + lax.rem(n, PICKS)]
        d = (place_ref[0] - lax.shift_right_logical(p, 3)) & (NZ - 1)
        h = lax.shift_right_logical(p, 2) & 1
        start = pl.multiple_of((p & 3) * ROWS, ROWS)
        to = pl.multiple_of(n * ROWS, ROWS)

        def act(buf):
            pltpu.make_async_copy(
                buf.at[pl.ds(start, ROWS), :], out.at[pl.ds(to, ROWS), :], sem
            ).start()

        choose(bufs, d * 2 + h, act)
        return carry

    for copy in sides:
        copy.start()
    lax.fori_loop(0, PIECES * PICKS, step, 0)
    pltpu.make_async_copy(out, out, sem).wait()
    for copy in sides:
        copy.wait()


def pick_pieces(place, picks, bufs, prev, below, above):
    half = jax.ShapeDtypeStruct((WHALF // 2, below.shape[1]), jnp.bfloat16)
    whole = lambda s: pl.BlockSpec(s.shape, lambda i, place, picks: (0, 0))
    pieces = jax.ShapeDtypeStruct((PIECES * PART, 2 * HD), jnp.bfloat16)
    side = jax.ShapeDtypeStruct(below.shape, below.dtype)
    return pl.pallas_call(
        pick_kernel,
        grid_spec=pltpu.PrefetchScalarGridSpec(
            num_scalar_prefetch=2,
            grid=(1,),
            in_specs=[ANY] * (2 * NZ + 3),
            out_specs=[ANY, ANY, whole(pieces), whole(half), whole(half)],
            scratch_shapes=[pltpu.SemaphoreType.DMA(()), pltpu.SemaphoreType.DMA((2,))],
        ),
        out_shape=[side, side, pieces, half, half],
        input_output_aliases={3 + 2 * NZ: 0, 4 + 2 * NZ: 1},
        compiler_params=params(60),
        cost_estimate=cost(0, MIB),
        name="pick_pieces",
    )(place, picks, *bufs, prev, below, above)


def contract(a, b):
    return lax.dot_general(a, b, (((1,), (1,)), ((), ())), preferred_element_type=jnp.float32)


def row_max(xs):
    top = jnp.max(xs[0], axis=1, keepdims=True)
    for x in xs[1:]:
        top = jnp.maximum(top, jnp.max(x, axis=1, keepdims=True))
    return top


def save_state(out_ref, rows, acc, top):
    lane = lax.broadcasted_iota(jnp.int32, (STACK, HD), 1)
    out_ref[rows, :HD] = acc[:, :HD]
    out_ref[rows, HD:] = jnp.where(lane < HD // 2, acc[:, HD:], top)


def near_kernel(place_ref, q_ref, k_ref, v_ref, prev_ref, stacked_ref, out_ref, own_v, prev_v):
    ones = jnp.ones((BLOCK, HD), jnp.bfloat16)
    own_v[:, :HD] = v_ref[...]
    own_v[:, HD:] = ones
    prev_v[:, :HD] = prev_ref[:, HD:]
    prev_v[:, HD:] = ones
    key = lax.broadcasted_iota(jnp.int32, (STACK, BLOCK), 1)
    token = lax.rem(lax.broadcasted_iota(jnp.int32, (STACK, BLOCK), 0), TILE)
    pen = jnp.where(place_ref[4] == 0, FAR, 0.0)

    def scores(i):
        at = pl.multiple_of(((place_ref[3] + i) & (NX - 1)) * TILE, TILE)
        for g in range(QPK):
            rows = slice(i * STACK + g * TILE, i * STACK + (g + 1) * TILE)
            stacked_ref[rows, :] = q_ref[pl.ds(at, TILE), g * HD : (g + 1) * HD]
        q = stacked_ref[i * STACK : (i + 1) * STACK, :]
        own = jnp.where(key - token <= at, contract(q, k_ref[...]) * SCALE, -FAR)
        return own, contract(q, prev_ref[:, :HD]) * SCALE

    after = scores(0)
    for i in range(NX):
        own, prev = after
        if i + 1 < NX:
            after = scores(i + 1)
        top = jnp.maximum(row_max([own]), row_max([prev]) - pen)
        own = jnp.exp2(own - top).astype(jnp.bfloat16)
        prev = jnp.exp2(prev - (top + pen)).astype(jnp.bfloat16)
        acc = jnp.dot(own, own_v[...], preferred_element_type=jnp.float32)
        acc += jnp.dot(prev, prev_v[...], preferred_element_type=jnp.float32)
        save_state(out_ref, slice(i * STACK, (i + 1) * STACK), acc, top)


def near_attention(place, q, k, v, prev):
    whole = lambda *shape: pl.BlockSpec(shape, lambda i, place: (0, 0))
    return pl.pallas_call(
        near_kernel,
        grid_spec=pltpu.PrefetchScalarGridSpec(
            num_scalar_prefetch=1,
            grid=(1,),
            in_specs=[
                whole(BLOCK, QPK * HD),
                whole(BLOCK, HD),
                whole(BLOCK, HD),
                whole(BLOCK, 2 * HD),
            ],
            out_specs=[whole(NX * STACK, HD), whole(NX * STACK, 2 * HD)],
            scratch_shapes=[pltpu.VMEM((BLOCK, 2 * HD), jnp.bfloat16)] * 2,
        ),
        out_shape=[
            jax.ShapeDtypeStruct((NX * STACK, HD), jnp.bfloat16),
            jax.ShapeDtypeStruct((NX * STACK, 2 * HD), jnp.float32),
        ],
        compiler_params=params(),
        cost_estimate=cost(1 << 20, MIB),
        name="near_attention",
    )(place, q, k, v, prev)


def summary_kernel(place_ref, q_ref, *refs):
    means, (out_ref, mean_k, mean_v) = refs[: 2 * NZ], refs[2 * NZ :]
    z, block = place_ref[0], place_ref[4]
    for s, mean in enumerate(means):
        rows = slice(s * MEAN_ROWS, (s + 1) * MEAN_ROWS)
        mean_k[rows, :] = mean[:, :HD]
        mean_v[rows, :HD] = mean[:, HD:]
    mean_v[:, HD:] = jnp.ones((2 * NZ * MEAN_ROWS, HD), jnp.bfloat16)

    s = lax.broadcasted_iota(jnp.int32, (1, 2 * NZ * MEAN_ROWS), 1)
    i4 = s & (MEAN_ROWS - 1)
    half = lax.shift_right_logical(s, 4) & 1
    zs = (z - lax.shift_right_logical(s, 5)) & (NZ - 1)
    number = zs * PIECES + half * (PIECES // 2) + i4
    bias = jnp.where((i4 < PIECES // 2) & (number < block), 0.0, -FAR)

    def scores(i):
        return contract(q_ref[i * STACK : (i + 1) * STACK, :], mean_k[...]) * SCALE + bias

    after = scores(0)
    for i in range(NX):
        sums = after
        if i + 1 < NX:
            after = scores(i + 1)
        top = jnp.maximum(row_max([sums]), 0.0)
        w = jnp.exp2(sums - top).astype(jnp.bfloat16)
        summary = jnp.dot(w, mean_v[...], preferred_element_type=jnp.float32)
        total = summary[:, HD:] + jnp.exp2(-top)
        out_ref[i * STACK : (i + 1) * STACK, :] = summary[:, :HD] / total


def summary_attention(place, q, bufs):
    whole = lambda rows, columns, at: pl.BlockSpec((rows, columns), lambda i, place: (at, 0))
    mean_count = 2 * NZ * MEAN_ROWS
    return pl.pallas_call(
        summary_kernel,
        grid_spec=pltpu.PrefetchScalarGridSpec(
            num_scalar_prefetch=1,
            grid=(1,),
            in_specs=[whole(NX * STACK, HD, 0)]
            + [whole(MEAN_ROWS, 2 * HD, HALF // MEAN_ROWS)] * (2 * NZ),
            out_specs=whole(NX * STACK, HD, 0),
            scratch_shapes=[
                pltpu.VMEM((mean_count, HD), jnp.bfloat16),
                pltpu.VMEM((mean_count, 2 * HD), jnp.bfloat16),
            ],
        ),
        out_shape=jax.ShapeDtypeStruct((NX * STACK, HD), jnp.float32),
        compiler_params=params(60),
        cost_estimate=cost(1 << 20, MIB),
        name="summary_attention",
    )(place, q, *bufs)


def far_values(place_ref, picks_ref, pieces_ref, v_all):
    block = place_ref[4]
    own = block & (PIECES - 1)
    for j in range(PICKS):
        p = picks_ref[own, j + 1]
        bad = p == block
        for e in range(j + 1):
            bad = bad | (p == picks_ref[own, e])
        keep = jnp.where(bad, 0.0, 1.0)
        ones = jnp.full((ROWS, HD), keep, jnp.float32).astype(jnp.bfloat16)
        for s in range(PIECES):
            at = slice(s * PART + j * ROWS, s * PART + (j + 1) * ROWS)
            v_all[at, :HD] = (pieces_ref[at, HD:].astype(jnp.float32) * keep).astype(jnp.bfloat16)
            v_all[at, HD:] = ones


def far_tiles(qs, states, pieces_ref, v_all, finish):
    chunks = [slice(n * BLOCK, (n + 1) * BLOCK) for n in range(PIECES * PART // BLOCK)]

    def scores(n):
        q = qs[n][...]
        return [contract(q, pieces_ref[chunk, :HD]) for chunk in chunks]

    after = scores(0)
    for n in range(len(qs)):
        xs = after
        if n + 1 < len(qs):
            after = scores(n + 1)
        state = states[n][...]
        top0 = state[:, 2 * HD - 1 :]
        top = jnp.maximum(top0, row_max(xs) * SCALE)
        acc = state * jnp.exp2(top0 - top)
        for chunk, x in zip(chunks, xs):
            w = jnp.exp2(x * SCALE - top).astype(jnp.bfloat16)
            acc += jnp.dot(w, v_all[chunk, :], preferred_element_type=jnp.float32)
        finish(n, acc, top)


def tile_spec(columns, at):
    return pl.BlockSpec((STACK, columns), lambda i, place, picks: (at, 0))


def whole_spec(rows, columns):
    return pl.BlockSpec((rows, columns), lambda i, place, picks: (0, 0))


def far_kernel(place_ref, picks_ref, q_ref, state_ref, summary_ref, pieces_ref, out_ref, v_all):
    tiles = [slice(n * STACK, (n + 1) * STACK) for n in range(NX)]

    def finish(n, acc, top):
        result = acc[:, :HD] / acc[:, HD : HD + 1] + summary_ref[tiles[n], :]
        result = result.astype(jnp.bfloat16)
        at = pl.multiple_of(((place_ref[3] + n) & (NX - 1)) * TILE, TILE)
        for g in range(QPK):
            out_ref[pl.ds(at, TILE), g * HD : (g + 1) * HD] = result[g * TILE : (g + 1) * TILE]

    @pl.when(place_ref[4] == 0)
    def _():
        for n in range(NX):
            finish(n, state_ref[tiles[n], :], None)

    @pl.when(place_ref[4] > 0)
    def _():
        far_values(place_ref, picks_ref, pieces_ref, v_all)
        far_tiles(
            [q_ref.at[t, :] for t in tiles],
            [state_ref.at[t, :] for t in tiles],
            pieces_ref,
            v_all,
            finish,
        )


def far_attention(place, picks, q, state, summary, pieces):
    whole = lambda *shape: pl.BlockSpec(shape, lambda i, place, picks: (0, 0))
    return pl.pallas_call(
        far_kernel,
        grid_spec=pltpu.PrefetchScalarGridSpec(
            num_scalar_prefetch=2,
            grid=(1,),
            in_specs=[
                whole(NX * STACK, HD),
                whole(NX * STACK, 2 * HD),
                whole(NX * STACK, HD),
                whole(PIECES * PART, 2 * HD),
            ],
            out_specs=whole(BLOCK, QPK * HD),
            scratch_shapes=[pltpu.VMEM((PIECES * PART, 2 * HD), jnp.bfloat16)],
        ),
        out_shape=jax.ShapeDtypeStruct((BLOCK, QPK * HD), jnp.bfloat16),
        compiler_params=params(),
        cost_estimate=cost(1 << 20, MIB),
        name="far_attention",
    )(place, picks, q, state, summary, pieces)


def hold_kernel(after_ref, low_ref, high_ref, low_out, high_out):
    pass


def hold(after, low, high):
    return pl.pallas_call(
        hold_kernel,
        in_specs=[ANY] * 3,
        out_specs=[ANY] * 2,
        out_shape=[jax.ShapeDtypeStruct(low.shape, low.dtype)] * 2,
        input_output_aliases={1: 0, 2: 1},
        compiler_params=params(16),
        cost_estimate=cost(0, 0),
        name="hold",
    )(after, low, high)


def project_kernel(place_ref, att_ref, w0, *refs):
    out_ref = refs[-1]
    x, c = place_ref[3], place_ref[2]
    depth = QPK * HD

    def columns(by, start, width):
        at = ((x + by) & (NX - 1)) * depth + start
        return att_ref[:, pl.ds(pl.multiple_of(at, width), width)]

    acc = jnp.dot(columns(0, 0, depth), w0[...], preferred_element_type=jnp.float32)
    for core, (below, above, low, high) in ((c, refs[:4]), (1 - c, refs[4:8])):
        opposite = jnp.concatenate([low[...], high[...]], axis=0)
        for by, w in ((-1, below[...]), (1, above[...]), (2, opposite)):
            a = columns(by, core * WHALF, WHALF)
            acc += jnp.dot(a, w, preferred_element_type=jnp.float32)
    out_ref[...] = acc.astype(jnp.bfloat16)


def project(place, attended, w0, weights):
    width, tile = w0.shape[1], 1024
    return pl.pallas_call(
        project_kernel,
        grid_spec=pltpu.PrefetchScalarGridSpec(
            num_scalar_prefetch=1,
            grid=(width // tile,),
            in_specs=[pl.BlockSpec((TILE, NX * QPK * HD), lambda n, place: (0, 0))]
            + [pl.BlockSpec((w.shape[0], tile), lambda n, place: (0, n)) for w in (w0, *weights)],
            out_specs=pl.BlockSpec((TILE, tile), lambda n, place: (0, n)),
        ),
        out_shape=jax.ShapeDtypeStruct((TILE, width), jnp.bfloat16),
        compiler_params=params(),
        cost_estimate=cost(1 << 20, MIB),
        name="project",
    )(place, attended, w0, *weights)


def shift(x, axis, size, by):
    return lax.ppermute(x, axis, [(i, (i + by) % size) for i in range(size)])


def swap(x):
    return lax.ppermute(x, "c", [(0, 1), (1, 0)])


def to_plane(x):
    return lax.all_to_all(x, ("y", "c"), 0, 0, tiled=True)


def per_device(q, k, v, picks, w):
    z, y, c, x = (lax.axis_index(a).astype(jnp.int32) for a in ("z", "y", "c", "x"))
    place = jnp.stack([z, y, c, x, z * PIECES + y * NC + c])
    plane_picks = lax.dynamic_slice_in_dim(picks.reshape(picks.shape[0], -1), z * PIECES, PIECES, 0)

    half = lax.dynamic_slice_in_dim(w, c * WHALF, WHALF, 0)
    sides = [shift(half, "x", NX, 1), shift(half, "x", NX, -1)]

    kv, msg = pack(k, v)
    a, b = unpack(to_plane(msg))
    blocks = NZ * PIECES
    prev = lax.ppermute(kv, ("z", "y", "c"), [(i, i + 1) for i in range(blocks - 1)])

    up, down = [(a, b)], [(a, b)]
    for d in range(3):
        up.append(tuple(shift(h, "z", NZ, 1) for h in up[-1]))
        down.append(tuple(shift(h, "z", NZ, -1) for h in down[-1]))
    far = (shift(up[3][0], "z", NZ, 1), shift(down[3][1], "z", NZ, -1))
    rings = up + [far] + [down[3], down[2], down[1]]
    bufs = [h for pair in rings for h in pair]

    below, above, pieces, low, high = pick_pieces(place, plane_picks, bufs, prev, *sides)
    pieces = to_plane(pieces)
    low, high = shift(low, "x", NX, 1), shift(high, "x", NX, -1)
    stacked, state = near_attention(place, q, k, v, prev)
    summary = summary_attention(place, stacked, bufs)
    attended = far_attention(place, plane_picks, stacked, state, summary, pieces)
    low, high = hold(attended, low, high)

    rows = lax.all_to_all(attended.reshape(NX, TILE, QPK * HD), "x", 0, 0, tiled=True)
    rows = jnp.transpose(rows, (1, 0, 2)).reshape(TILE, NX * QPK * HD)
    weights = [below, above, low, high]
    return project(place, rows, w, weights + [swap(m) for m in weights])


def solution(mesh):
    fine = Mesh(mesh.devices.reshape(NZ, NY, NC, NX), ("z", "y", "c", "x"))
    ctx = ("z", "y", "c")
    in_specs = (P(ctx, "x"), P(ctx, "x"), P(ctx, "x"), P(None, "x", None), P("x", None))
    out_specs = P(("z", "y", "c", "x"), None)
    return jax.shard_map(
        per_device, mesh=fine, in_specs=in_specs, out_specs=out_specs, check_vma=False
    )
```

```python
import functools
import math

import jax
import jax.numpy as jnp
from jax import lax
from jax.experimental import pallas as pl
from jax.experimental.pallas import tpu as pltpu
from jax.sharding import Mesh
from jax.sharding import PartitionSpec as P

HD = 128
BLOCK = 512
QPK = 4
PICKS = 6
PIECES = 8
ROWS = BLOCK // PIECES
PART = PICKS * ROWS
MEAN_ROWS = 16
MSG = ROWS + MEAN_ROWS
HALF = PIECES // 2 * ROWS
NZ, NY, NC, NX = 8, 4, 2, 4
TILE = BLOCK // NX
STACK = TILE * QPK
SCALE = HD**-0.5 * math.log2(math.e)
WHALF = QPK * HD // NC
FAR = 1e30
MIB = 1 << 20

ANY = pl.BlockSpec(memory_space=pl.ANY)


def params(mib=40):
    return pltpu.CompilerParams(vmem_limit_bytes=mib * MIB)


def cost(flops, nbytes, trans=0):
    return pl.CostEstimate(flops=flops, bytes_accessed=nbytes, transcendentals=trans)


def pack_kernel(k_ref, v_ref, kv_ref, msg_ref):
    k = k_ref[...]
    v = v_ref[...]
    kv_ref[:, :HD] = k
    kv_ref[:, HD:] = v
    mk = jnp.sum(k.astype(jnp.float32), axis=0, keepdims=True) * (1.0 / BLOCK)
    mv = jnp.sum(v.astype(jnp.float32), axis=0, keepdims=True) * (1.0 / BLOCK)
    mean = jnp.concatenate([mk, mv], axis=1).astype(jnp.bfloat16)
    mean = jnp.broadcast_to(mean, (MEAN_ROWS, 2 * HD))
    for r in range(PIECES):
        rows = slice(r * ROWS, (r + 1) * ROWS)
        msg_ref[r, :ROWS, :HD] = k_ref[rows, :]
        msg_ref[r, :ROWS, HD:] = v_ref[rows, :]
        msg_ref[r, ROWS:, :] = mean


def pack(k, v):
    return pl.pallas_call(
        pack_kernel,
        out_shape=[
            jax.ShapeDtypeStruct((BLOCK, 2 * HD), jnp.bfloat16),
            jax.ShapeDtypeStruct((PIECES, MSG, 2 * HD), jnp.bfloat16),
        ],
        compiler_params=params(16),
        cost_estimate=cost(1 << 18, MIB),
        name="pack",
    )(k, v)


def unpack_kernel(msg_ref, a_ref, b_ref):
    row = lax.broadcasted_iota(jnp.int32, (MEAN_ROWS, 2 * HD), 0)
    for h, out in enumerate((a_ref, b_ref)):
        means = jnp.zeros((MEAN_ROWS, 2 * HD), jnp.float32)
        for i in range(PIECES // 2):
            s = h * (PIECES // 2) + i
            out[i * ROWS : (i + 1) * ROWS, :] = msg_ref[s, :ROWS, :]
            means = jnp.where(row == i, msg_ref[s, ROWS:, :].astype(jnp.float32), means)
        out[HALF:, :] = means.astype(jnp.bfloat16)


def unpack(msg):
    return pl.pallas_call(
        unpack_kernel,
        out_shape=[jax.ShapeDtypeStruct((HALF + MEAN_ROWS, 2 * HD), jnp.bfloat16)] * 2,
        compiler_params=params(16),
        cost_estimate=cost(1 << 18, MIB),
        name="unpack",
    )(msg)


def choose(refs, index, act):
    if len(refs) == 1:
        act(refs[0])
        return
    half = len(refs) // 2
    pl.when(index < half)(lambda: choose(refs[:half], index, act))
    pl.when(index >= half)(lambda: choose(refs[half:], index - half, act))


def pick_kernel(place_ref, picks_ref, *refs):
    bufs, below, above = refs[: 2 * NZ], refs[2 * NZ + 1], refs[2 * NZ + 2]
    out, low, high, sem, side_sem = refs[-5:]
    rows = WHALF // 2
    sides = [
        pltpu.make_async_copy(below.at[:rows, :], low, side_sem.at[0]),
        pltpu.make_async_copy(above.at[rows:, :], high, side_sem.at[1]),
    ]

    def step(n, carry):
        p = picks_ref[lax.div(n, PICKS), 1 + lax.rem(n, PICKS)]
        d = (place_ref[0] - lax.shift_right_logical(p, 3)) & (NZ - 1)
        h = lax.shift_right_logical(p, 2) & 1
        start = pl.multiple_of((p & 3) * ROWS, ROWS)
        to = pl.multiple_of(n * ROWS, ROWS)

        def act(buf):
            pltpu.make_async_copy(
                buf.at[pl.ds(start, ROWS), :], out.at[pl.ds(to, ROWS), :], sem
            ).start()

        choose(bufs, d * 2 + h, act)
        return carry

    for copy in sides:
        copy.start()
    lax.fori_loop(0, PIECES * PICKS, step, 0)
    pltpu.make_async_copy(out, out, sem).wait()
    for copy in sides:
        copy.wait()


def pick_pieces(place, picks, bufs, prev, below, above):
    half = jax.ShapeDtypeStruct((WHALF // 2, below.shape[1]), jnp.bfloat16)
    whole = lambda s: pl.BlockSpec(s.shape, lambda i, place, picks: (0, 0))
    pieces = jax.ShapeDtypeStruct((PIECES * PART, 2 * HD), jnp.bfloat16)
    side = jax.ShapeDtypeStruct(below.shape, below.dtype)
    return pl.pallas_call(
        pick_kernel,
        grid_spec=pltpu.PrefetchScalarGridSpec(
            num_scalar_prefetch=2,
            grid=(1,),
            in_specs=[ANY] * (2 * NZ + 3),
            out_specs=[ANY, ANY, whole(pieces), whole(half), whole(half)],
            scratch_shapes=[pltpu.SemaphoreType.DMA(()), pltpu.SemaphoreType.DMA((2,))],
        ),
        out_shape=[side, side, pieces, half, half],
        input_output_aliases={3 + 2 * NZ: 0, 4 + 2 * NZ: 1},
        compiler_params=params(60),
        cost_estimate=cost(0, MIB),
        name="pick_pieces",
    )(place, picks, *bufs, prev, below, above)


def contract(a, b):
    return lax.dot_general(a, b, (((1,), (1,)), ((), ())), preferred_element_type=jnp.float32)


def row_max(xs):
    top = jnp.max(xs[0], axis=1, keepdims=True)
    for x in xs[1:]:
        top = jnp.maximum(top, jnp.max(x, axis=1, keepdims=True))
    return top


def save_state(out_ref, rows, acc, top):
    lane = lax.broadcasted_iota(jnp.int32, (STACK, HD), 1)
    out_ref[rows, :HD] = acc[:, :HD]
    out_ref[rows, HD:] = jnp.where(lane < HD // 2, acc[:, HD:], top)


def near_kernel(place_ref, q_ref, k_ref, v_ref, prev_ref, stacked_ref, out_ref, own_v, prev_v):
    ones = jnp.ones((BLOCK, HD), jnp.bfloat16)
    own_v[:, :HD] = v_ref[...]
    own_v[:, HD:] = ones
    prev_v[:, :HD] = prev_ref[:, HD:]
    prev_v[:, HD:] = ones
    key = lax.broadcasted_iota(jnp.int32, (STACK, BLOCK), 1)
    token = lax.rem(lax.broadcasted_iota(jnp.int32, (STACK, BLOCK), 0), TILE)
    pen = jnp.where(place_ref[4] == 0, FAR, 0.0)

    def scores(i):
        at = pl.multiple_of(((place_ref[3] + i) & (NX - 1)) * TILE, TILE)
        for g in range(QPK):
            rows = slice(i * STACK + g * TILE, i * STACK + (g + 1) * TILE)
            stacked_ref[rows, :] = q_ref[pl.ds(at, TILE), g * HD : (g + 1) * HD]
        q = stacked_ref[i * STACK : (i + 1) * STACK, :]
        own = jnp.where(key - token <= at, contract(q, k_ref[...]) * SCALE, -FAR)
        return own, contract(q, prev_ref[:, :HD]) * SCALE

    after = scores(0)
    for i in range(NX):
        own, prev = after
        if i + 1 < NX:
            after = scores(i + 1)
        top = jnp.maximum(row_max([own]), row_max([prev]) - pen)
        own = jnp.exp2(own - top).astype(jnp.bfloat16)
        prev = jnp.exp2(prev - (top + pen)).astype(jnp.bfloat16)
        acc = jnp.dot(own, own_v[...], preferred_element_type=jnp.float32)
        acc += jnp.dot(prev, prev_v[...], preferred_element_type=jnp.float32)
        save_state(out_ref, slice(i * STACK, (i + 1) * STACK), acc, top)


def near_attention(place, q, k, v, prev):
    whole = lambda *shape: pl.BlockSpec(shape, lambda i, place: (0, 0))
    return pl.pallas_call(
        near_kernel,
        grid_spec=pltpu.PrefetchScalarGridSpec(
            num_scalar_prefetch=1,
            grid=(1,),
            in_specs=[
                whole(BLOCK, QPK * HD),
                whole(BLOCK, HD),
                whole(BLOCK, HD),
                whole(BLOCK, 2 * HD),
            ],
            out_specs=[whole(NX * STACK, HD), whole(NX * STACK, 2 * HD)],
            scratch_shapes=[pltpu.VMEM((BLOCK, 2 * HD), jnp.bfloat16)] * 2,
        ),
        out_shape=[
            jax.ShapeDtypeStruct((NX * STACK, HD), jnp.bfloat16),
            jax.ShapeDtypeStruct((NX * STACK, 2 * HD), jnp.float32),
        ],
        compiler_params=params(),
        cost_estimate=cost(1 << 20, MIB),
        name="near_attention",
    )(place, q, k, v, prev)


def summary_kernel(place_ref, q_ref, *refs):
    means, (out_ref, mean_k, mean_v) = refs[: 2 * NZ], refs[2 * NZ :]
    z, block = place_ref[0], place_ref[4]
    for s, mean in enumerate(means):
        rows = slice(s * MEAN_ROWS, (s + 1) * MEAN_ROWS)
        mean_k[rows, :] = mean[:, :HD]
        mean_v[rows, :HD] = mean[:, HD:]
    mean_v[:, HD:] = jnp.ones((2 * NZ * MEAN_ROWS, HD), jnp.bfloat16)

    s = lax.broadcasted_iota(jnp.int32, (1, 2 * NZ * MEAN_ROWS), 1)
    i4 = s & (MEAN_ROWS - 1)
    half = lax.shift_right_logical(s, 4) & 1
    zs = (z - lax.shift_right_logical(s, 5)) & (NZ - 1)
    number = zs * PIECES + half * (PIECES // 2) + i4
    bias = jnp.where((i4 < PIECES // 2) & (number < block), 0.0, -FAR)

    def scores(i):
        return contract(q_ref[i * STACK : (i + 1) * STACK, :], mean_k[...]) * SCALE + bias

    after = scores(0)
    for i in range(NX):
        sums = after
        if i + 1 < NX:
            after = scores(i + 1)
        top = jnp.maximum(row_max([sums]), 0.0)
        w = jnp.exp2(sums - top).astype(jnp.bfloat16)
        summary = jnp.dot(w, mean_v[...], preferred_element_type=jnp.float32)
        total = summary[:, HD:] + jnp.exp2(-top)
        out_ref[i * STACK : (i + 1) * STACK, :] = summary[:, :HD] / total


def summary_attention(place, q, bufs):
    whole = lambda rows, columns, at: pl.BlockSpec((rows, columns), lambda i, place: (at, 0))
    mean_count = 2 * NZ * MEAN_ROWS
    return pl.pallas_call(
        summary_kernel,
        grid_spec=pltpu.PrefetchScalarGridSpec(
            num_scalar_prefetch=1,
            grid=(1,),
            in_specs=[whole(NX * STACK, HD, 0)]
            + [whole(MEAN_ROWS, 2 * HD, HALF // MEAN_ROWS)] * (2 * NZ),
            out_specs=whole(NX * STACK, HD, 0),
            scratch_shapes=[
                pltpu.VMEM((mean_count, HD), jnp.bfloat16),
                pltpu.VMEM((mean_count, 2 * HD), jnp.bfloat16),
            ],
        ),
        out_shape=jax.ShapeDtypeStruct((NX * STACK, HD), jnp.float32),
        compiler_params=params(60),
        cost_estimate=cost(1 << 20, MIB),
        name="summary_attention",
    )(place, q, *bufs)


def far_values(place_ref, picks_ref, pieces_ref, v_all):
    block = place_ref[4]
    own = block & (PIECES - 1)
    for j in range(PICKS):
        p = picks_ref[own, j + 1]
        bad = p == block
        for e in range(j + 1):
            bad = bad | (p == picks_ref[own, e])
        keep = jnp.where(bad, 0.0, 1.0)
        ones = jnp.full((ROWS, HD), keep, jnp.float32).astype(jnp.bfloat16)
        for s in range(PIECES):
            at = slice(s * PART + j * ROWS, s * PART + (j + 1) * ROWS)
            v_all[at, :HD] = (pieces_ref[at, HD:].astype(jnp.float32) * keep).astype(jnp.bfloat16)
            v_all[at, HD:] = ones


def far_kernel(
    place_ref,
    picks_ref,
    q_ref,
    pieces_ref,
    state_hbm,
    summary_hbm,
    out_ref,
    v_all,
    state_ref,
    summary_ref,
    sems,
):
    tiles = [pl.ds(n * STACK, STACK) for n in range(NX)]
    copies = []
    for n, tile in enumerate(tiles):
        copies.append(
            (
                pltpu.make_async_copy(state_hbm.at[tile, :], state_ref.at[tile, :], sems.at[0, n]),
                pltpu.make_async_copy(
                    summary_hbm.at[tile, :], summary_ref.at[tile, :], sems.at[1, n]
                ),
            )
        )
    for pair in copies:
        for copy in pair:
            copy.start()

    def arrive():
        for pair in copies:
            for copy in pair:
                copy.wait()

    def finish(n, acc):
        result = acc[:, :HD] / acc[:, HD : HD + 1] + summary_ref[tiles[n], :]
        result = result.astype(jnp.bfloat16)
        at = pl.multiple_of(((place_ref[3] + n) & (NX - 1)) * TILE, TILE)
        for g in range(QPK):
            out_ref[pl.ds(at, TILE), g * HD : (g + 1) * HD] = result[g * TILE : (g + 1) * TILE]

    @pl.when(place_ref[4] == 0)
    def _():
        arrive()
        for n in range(NX):
            finish(n, state_ref[tiles[n], :])

    @pl.when(place_ref[4] > 0)
    def _():
        chunks = [slice(n * BLOCK, (n + 1) * BLOCK) for n in range(PIECES * PART // BLOCK)]

        def scores(n):
            q = q_ref[tiles[n], :]
            return [contract(q, pieces_ref[chunk, :HD]) for chunk in chunks]

        far_values(place_ref, picks_ref, pieces_ref, v_all)
        arrive()
        after = scores(0)
        for n in range(NX):
            xs = after
            if n + 1 < NX:
                after = scores(n + 1)
            state = state_ref[tiles[n], :]
            top0 = state[:, 2 * HD - 1 :]
            top = jnp.maximum(top0, row_max(xs) * SCALE)
            acc = state * jnp.exp2(top0 - top)
            for chunk, x in zip(chunks, xs):
                w = jnp.exp2(x * SCALE - top).astype(jnp.bfloat16)
                acc += jnp.dot(w, v_all[chunk, :], preferred_element_type=jnp.float32)
            finish(n, acc)


def far_attention(place, picks, q, state, summary, pieces):
    whole = lambda *shape: pl.BlockSpec(shape, lambda i, place, picks: (0, 0))
    return pl.pallas_call(
        far_kernel,
        grid_spec=pltpu.PrefetchScalarGridSpec(
            num_scalar_prefetch=2,
            grid=(1,),
            in_specs=[whole(NX * STACK, HD), whole(PIECES * PART, 2 * HD), ANY, ANY],
            out_specs=whole(BLOCK, QPK * HD),
            scratch_shapes=[
                pltpu.VMEM((PIECES * PART, 2 * HD), jnp.bfloat16),
                pltpu.VMEM((NX * STACK, 2 * HD), jnp.float32),
                pltpu.VMEM((NX * STACK, HD), jnp.float32),
                pltpu.SemaphoreType.DMA((2, NX)),
            ],
        ),
        out_shape=jax.ShapeDtypeStruct((BLOCK, QPK * HD), jnp.bfloat16),
        compiler_params=params(60),
        cost_estimate=cost(1 << 20, MIB),
        name="far_attention",
    )(place, picks, q, pieces, state, summary)


def hold_kernel(after_ref, low_ref, high_ref, low_out, high_out):
    pass


def hold(after, low, high):
    return pl.pallas_call(
        hold_kernel,
        in_specs=[ANY] * 3,
        out_specs=[ANY] * 2,
        out_shape=[jax.ShapeDtypeStruct(low.shape, low.dtype)] * 2,
        input_output_aliases={1: 0, 2: 1},
        compiler_params=params(16),
        cost_estimate=cost(0, 0),
        name="hold",
    )(after, low, high)


def project_kernel(place_ref, att_ref, w0, *refs):
    out_ref = refs[-1]
    x, c = place_ref[3], place_ref[2]
    depth = QPK * HD

    def columns(by, start, width):
        at = ((x + by) & (NX - 1)) * depth + start
        return att_ref[:, pl.ds(pl.multiple_of(at, width), width)]

    acc = jnp.dot(columns(0, 0, depth), w0[...], preferred_element_type=jnp.float32)
    for core, (below, above, low, high) in ((c, refs[:4]), (1 - c, refs[4:8])):
        opposite = jnp.concatenate([low[...], high[...]], axis=0)
        for by, w in ((-1, below[...]), (1, above[...]), (2, opposite)):
            a = columns(by, core * WHALF, WHALF)
            acc += jnp.dot(a, w, preferred_element_type=jnp.float32)
    out_ref[...] = acc.astype(jnp.bfloat16)


def project(place, attended, w0, weights):
    width, tile = w0.shape[1], 1024
    return pl.pallas_call(
        project_kernel,
        grid_spec=pltpu.PrefetchScalarGridSpec(
            num_scalar_prefetch=1,
            grid=(width // tile,),
            in_specs=[pl.BlockSpec((TILE, NX * QPK * HD), lambda n, place: (0, 0))]
            + [pl.BlockSpec((w.shape[0], tile), lambda n, place: (0, n)) for w in (w0, *weights)],
            out_specs=pl.BlockSpec((TILE, tile), lambda n, place: (0, n)),
        ),
        out_shape=jax.ShapeDtypeStruct((TILE, width), jnp.bfloat16),
        compiler_params=params(),
        cost_estimate=cost(1 << 20, MIB),
        name="project",
    )(place, attended, w0, *weights)


def shift(x, axis, size, by):
    return lax.ppermute(x, axis, [(i, (i + by) % size) for i in range(size)])


def swap(x):
    return lax.ppermute(x, "c", [(0, 1), (1, 0)])


def to_plane(x):
    return lax.all_to_all(x, ("y", "c"), 0, 0, tiled=True)


def per_device(q, k, v, picks, w):
    z, y, c, x = (lax.axis_index(a).astype(jnp.int32) for a in ("z", "y", "c", "x"))
    place = jnp.stack([z, y, c, x, z * PIECES + y * NC + c])
    plane_picks = lax.dynamic_slice_in_dim(picks.reshape(picks.shape[0], -1), z * PIECES, PIECES, 0)

    half = lax.dynamic_slice_in_dim(w, c * WHALF, WHALF, 0)
    sides = [shift(half, "x", NX, 1), shift(half, "x", NX, -1)]

    kv, msg = pack(k, v)
    a, b = unpack(to_plane(msg))
    blocks = NZ * PIECES
    prev = lax.ppermute(kv, ("z", "y", "c"), [(i, i + 1) for i in range(blocks - 1)])

    up, down = [(a, b)], [(a, b)]
    for d in range(3):
        up.append(tuple(shift(h, "z", NZ, 1) for h in up[-1]))
        down.append(tuple(shift(h, "z", NZ, -1) for h in down[-1]))
    far = (shift(up[3][0], "z", NZ, 1), shift(down[3][1], "z", NZ, -1))
    rings = up + [far] + [down[3], down[2], down[1]]
    bufs = [h for pair in rings for h in pair]

    below, above, pieces, low, high = pick_pieces(place, plane_picks, bufs, prev, *sides)
    pieces = to_plane(pieces)
    low, high = shift(low, "x", NX, 1), shift(high, "x", NX, -1)
    stacked, state = near_attention(place, q, k, v, prev)
    summary = summary_attention(place, stacked, bufs)
    attended = far_attention(place, plane_picks, stacked, state, summary, pieces)
    low, high = hold(attended, low, high)

    rows = lax.all_to_all(attended.reshape(NX, TILE, QPK * HD), "x", 0, 0, tiled=True)
    rows = jnp.transpose(rows, (1, 0, 2)).reshape(TILE, NX * QPK * HD)
    weights = [below, above, low, high]
    return project(place, rows, w, weights + [swap(m) for m in weights])


def solution(mesh):
    fine = Mesh(mesh.devices.reshape(NZ, NY, NC, NX), ("z", "y", "c", "x"))
    ctx = ("z", "y", "c")
    in_specs = (P(ctx, "x"), P(ctx, "x"), P(ctx, "x"), P(None, "x", None), P("x", None))
    out_specs = P(("z", "y", "c", "x"), None)
    return jax.shard_map(
        per_device, mesh=fine, in_specs=in_specs, out_specs=out_specs, check_vma=False
    )
```

```python
import functools
import math

import jax
import jax.numpy as jnp
from jax import lax
from jax.experimental import pallas as pl
from jax.experimental.pallas import tpu as pltpu
from jax.sharding import Mesh
from jax.sharding import PartitionSpec as P

HD = 128
BLOCK = 512
QPK = 4
PICKS = 6
PIECES = 8
ROWS = BLOCK // PIECES
PART = PICKS * ROWS
MEAN_ROWS = 16
MSG = ROWS + MEAN_ROWS
HALF = PIECES // 2 * ROWS
NZ, NY, NC, NX = 8, 4, 2, 4
TILE = BLOCK // NX
STACK = TILE * QPK
SCALE = HD**-0.5 * math.log2(math.e)
WHALF = QPK * HD // NC
FAR = 1e30
MIB = 1 << 20

ANY = pl.BlockSpec(memory_space=pl.ANY)


def params(mib=40):
    return pltpu.CompilerParams(vmem_limit_bytes=mib * MIB)


def cost(flops, nbytes, trans=0):
    return pl.CostEstimate(flops=flops, bytes_accessed=nbytes, transcendentals=trans)


def pack_kernel(k_ref, v_ref, kv_ref, msg_ref):
    k = k_ref[...]
    v = v_ref[...]
    kv_ref[:, :HD] = k
    kv_ref[:, HD:] = v
    mk = jnp.sum(k.astype(jnp.float32), axis=0, keepdims=True) * (1.0 / BLOCK)
    mv = jnp.sum(v.astype(jnp.float32), axis=0, keepdims=True) * (1.0 / BLOCK)
    mean = jnp.concatenate([mk, mv], axis=1).astype(jnp.bfloat16)
    mean = jnp.broadcast_to(mean, (MEAN_ROWS, 2 * HD))
    for r in range(PIECES):
        rows = slice(r * ROWS, (r + 1) * ROWS)
        msg_ref[r, :ROWS, :HD] = k_ref[rows, :]
        msg_ref[r, :ROWS, HD:] = v_ref[rows, :]
        msg_ref[r, ROWS:, :] = mean


def pack(k, v):
    return pl.pallas_call(
        pack_kernel,
        out_shape=[
            jax.ShapeDtypeStruct((BLOCK, 2 * HD), jnp.bfloat16),
            jax.ShapeDtypeStruct((PIECES, MSG, 2 * HD), jnp.bfloat16),
        ],
        compiler_params=params(16),
        cost_estimate=cost(1 << 18, MIB),
        name="pack",
    )(k, v)


def unpack_kernel(msg_ref, a_ref, b_ref):
    row = lax.broadcasted_iota(jnp.int32, (MEAN_ROWS, 2 * HD), 0)
    for h, out in enumerate((a_ref, b_ref)):
        means = jnp.zeros((MEAN_ROWS, 2 * HD), jnp.float32)
        for i in range(PIECES // 2):
            s = h * (PIECES // 2) + i
            out[i * ROWS : (i + 1) * ROWS, :] = msg_ref[s, :ROWS, :]
            means = jnp.where(row == i, msg_ref[s, ROWS:, :].astype(jnp.float32), means)
        out[HALF:, :] = means.astype(jnp.bfloat16)


def unpack(msg):
    return pl.pallas_call(
        unpack_kernel,
        out_shape=[jax.ShapeDtypeStruct((HALF + MEAN_ROWS, 2 * HD), jnp.bfloat16)] * 2,
        compiler_params=params(16),
        cost_estimate=cost(1 << 18, MIB),
        name="unpack",
    )(msg)


def choose(refs, index, act):
    if len(refs) == 1:
        act(refs[0])
        return
    half = len(refs) // 2
    pl.when(index < half)(lambda: choose(refs[:half], index, act))
    pl.when(index >= half)(lambda: choose(refs[half:], index - half, act))


def pick_kernel(place_ref, picks_ref, *refs):
    bufs, below, above = refs[: 2 * NZ], refs[2 * NZ + 1], refs[2 * NZ + 2]
    out, low, high, sem, side_sem = refs[-5:]
    rows = WHALF // 2
    sides = [
        pltpu.make_async_copy(below.at[:rows, :], low, side_sem.at[0]),
        pltpu.make_async_copy(above.at[rows:, :], high, side_sem.at[1]),
    ]

    def step(n, carry):
        p = picks_ref[lax.div(n, PICKS), 1 + lax.rem(n, PICKS)]
        d = (place_ref[0] - lax.shift_right_logical(p, 3)) & (NZ - 1)
        h = lax.shift_right_logical(p, 2) & 1
        start = pl.multiple_of((p & 3) * ROWS, ROWS)
        to = pl.multiple_of(n * ROWS, ROWS)

        def act(buf):
            pltpu.make_async_copy(
                buf.at[pl.ds(start, ROWS), :], out.at[pl.ds(to, ROWS), :], sem
            ).start()

        choose(bufs, d * 2 + h, act)
        return carry

    for copy in sides:
        copy.start()
    lax.fori_loop(0, PIECES * PICKS, step, 0, unroll=4)
    pltpu.make_async_copy(out, out, sem).wait()
    for copy in sides:
        copy.wait()


def pick_pieces(place, picks, bufs, prev, below, above):
    half = jax.ShapeDtypeStruct((WHALF // 2, below.shape[1]), jnp.bfloat16)
    whole = lambda s: pl.BlockSpec(s.shape, lambda i, place, picks: (0, 0))
    pieces = jax.ShapeDtypeStruct((PIECES * PART, 2 * HD), jnp.bfloat16)
    side = jax.ShapeDtypeStruct(below.shape, below.dtype)
    return pl.pallas_call(
        pick_kernel,
        grid_spec=pltpu.PrefetchScalarGridSpec(
            num_scalar_prefetch=2,
            grid=(1,),
            in_specs=[ANY] * (2 * NZ + 3),
            out_specs=[ANY, ANY, whole(pieces), whole(half), whole(half)],
            scratch_shapes=[pltpu.SemaphoreType.DMA(()), pltpu.SemaphoreType.DMA((2,))],
        ),
        out_shape=[side, side, pieces, half, half],
        input_output_aliases={3 + 2 * NZ: 0, 4 + 2 * NZ: 1},
        compiler_params=params(60),
        cost_estimate=cost(0, MIB),
        name="pick_pieces",
    )(place, picks, *bufs, prev, below, above)


def contract(a, b):
    return lax.dot_general(a, b, (((1,), (1,)), ((), ())), preferred_element_type=jnp.float32)


def row_max(xs):
    top = jnp.max(xs[0], axis=1, keepdims=True)
    for x in xs[1:]:
        top = jnp.maximum(top, jnp.max(x, axis=1, keepdims=True))
    return top


def save_state(out_ref, rows, acc, top):
    lane = lax.broadcasted_iota(jnp.int32, (STACK, HD), 1)
    out_ref[rows, :HD] = acc[:, :HD]
    out_ref[rows, HD:] = jnp.where(lane < HD // 2, acc[:, HD:], top)


def near_kernel(place_ref, q_ref, k_ref, v_ref, prev_ref, stacked_ref, out_ref, own_v, prev_v):
    ones = jnp.ones((BLOCK, HD), jnp.bfloat16)
    own_v[:, :HD] = v_ref[...]
    own_v[:, HD:] = ones
    prev_v[:, :HD] = prev_ref[:, HD:]
    prev_v[:, HD:] = ones
    key = lax.broadcasted_iota(jnp.int32, (STACK, BLOCK), 1)
    token = lax.rem(lax.broadcasted_iota(jnp.int32, (STACK, BLOCK), 0), TILE)
    pen = jnp.where(place_ref[4] == 0, FAR, 0.0)

    def scores(i):
        at = pl.multiple_of(((place_ref[3] + i) & (NX - 1)) * TILE, TILE)
        for g in range(QPK):
            rows = slice(i * STACK + g * TILE, i * STACK + (g + 1) * TILE)
            stacked_ref[rows, :] = q_ref[pl.ds(at, TILE), g * HD : (g + 1) * HD]
        q = stacked_ref[i * STACK : (i + 1) * STACK, :]
        own = jnp.where(key - token <= at, contract(q, k_ref[...]) * SCALE, -FAR)
        return own, contract(q, prev_ref[:, :HD]) * SCALE

    after = scores(0)
    for i in range(NX):
        own, prev = after
        if i + 1 < NX:
            after = scores(i + 1)
        top = jnp.maximum(row_max([own]), row_max([prev]) - pen)
        own = jnp.exp2(own - top).astype(jnp.bfloat16)
        prev = jnp.exp2(prev - (top + pen)).astype(jnp.bfloat16)
        acc = jnp.dot(own, own_v[...], preferred_element_type=jnp.float32)
        acc += jnp.dot(prev, prev_v[...], preferred_element_type=jnp.float32)
        save_state(out_ref, slice(i * STACK, (i + 1) * STACK), acc, top)


def near_attention(place, q, k, v, prev):
    whole = lambda *shape: pl.BlockSpec(shape, lambda i, place: (0, 0))
    return pl.pallas_call(
        near_kernel,
        grid_spec=pltpu.PrefetchScalarGridSpec(
            num_scalar_prefetch=1,
            grid=(1,),
            in_specs=[
                whole(BLOCK, QPK * HD),
                whole(BLOCK, HD),
                whole(BLOCK, HD),
                whole(BLOCK, 2 * HD),
            ],
            out_specs=[whole(NX * STACK, HD), whole(NX * STACK, 2 * HD)],
            scratch_shapes=[pltpu.VMEM((BLOCK, 2 * HD), jnp.bfloat16)] * 2,
        ),
        out_shape=[
            jax.ShapeDtypeStruct((NX * STACK, HD), jnp.bfloat16),
            jax.ShapeDtypeStruct((NX * STACK, 2 * HD), jnp.float32),
        ],
        compiler_params=params(),
        cost_estimate=cost(1 << 20, MIB),
        name="near_attention",
    )(place, q, k, v, prev)


def summary_kernel(place_ref, q_ref, *refs):
    means, (out_ref, mean_k, mean_v) = refs[: 2 * NZ], refs[2 * NZ :]
    z, block = place_ref[0], place_ref[4]
    for s, mean in enumerate(means):
        rows = slice(s * MEAN_ROWS, (s + 1) * MEAN_ROWS)
        mean_k[rows, :] = mean[:, :HD]
        mean_v[rows, :HD] = mean[:, HD:]
    mean_v[:, HD:] = jnp.ones((2 * NZ * MEAN_ROWS, HD), jnp.bfloat16)

    s = lax.broadcasted_iota(jnp.int32, (1, 2 * NZ * MEAN_ROWS), 1)
    i4 = s & (MEAN_ROWS - 1)
    half = lax.shift_right_logical(s, 4) & 1
    zs = (z - lax.shift_right_logical(s, 5)) & (NZ - 1)
    number = zs * PIECES + half * (PIECES // 2) + i4
    bias = jnp.where((i4 < PIECES // 2) & (number < block), 0.0, -FAR)

    def scores(i):
        return contract(q_ref[i * STACK : (i + 1) * STACK, :], mean_k[...]) * SCALE + bias

    after = scores(0)
    for i in range(NX):
        sums = after
        if i + 1 < NX:
            after = scores(i + 1)
        top = jnp.maximum(row_max([sums]), 0.0)
        w = jnp.exp2(sums - top).astype(jnp.bfloat16)
        summary = jnp.dot(w, mean_v[...], preferred_element_type=jnp.float32)
        total = summary[:, HD:] + jnp.exp2(-top)
        out_ref[i * STACK : (i + 1) * STACK, :] = summary[:, :HD] / total


def summary_attention(place, q, bufs):
    whole = lambda rows, columns, at: pl.BlockSpec((rows, columns), lambda i, place: (at, 0))
    mean_count = 2 * NZ * MEAN_ROWS
    return pl.pallas_call(
        summary_kernel,
        grid_spec=pltpu.PrefetchScalarGridSpec(
            num_scalar_prefetch=1,
            grid=(1,),
            in_specs=[whole(NX * STACK, HD, 0)]
            + [whole(MEAN_ROWS, 2 * HD, HALF // MEAN_ROWS)] * (2 * NZ),
            out_specs=whole(NX * STACK, HD, 0),
            scratch_shapes=[
                pltpu.VMEM((mean_count, HD), jnp.bfloat16),
                pltpu.VMEM((mean_count, 2 * HD), jnp.bfloat16),
            ],
        ),
        out_shape=jax.ShapeDtypeStruct((NX * STACK, HD), jnp.float32),
        compiler_params=params(60),
        cost_estimate=cost(1 << 20, MIB),
        name="summary_attention",
    )(place, q, *bufs)


def far_values(place_ref, picks_ref, pieces_ref, v_all):
    block = place_ref[4]
    own = block & (PIECES - 1)
    for j in range(PICKS):
        p = picks_ref[own, j + 1]
        bad = p == block
        for e in range(j + 1):
            bad = bad | (p == picks_ref[own, e])
        keep = jnp.where(bad, 0.0, 1.0)
        ones = jnp.full((ROWS, HD), keep, jnp.float32).astype(jnp.bfloat16)
        for s in range(PIECES):
            at = slice(s * PART + j * ROWS, s * PART + (j + 1) * ROWS)
            v_all[at, :HD] = (pieces_ref[at, HD:].astype(jnp.float32) * keep).astype(jnp.bfloat16)
            v_all[at, HD:] = ones


def far_kernel(
    place_ref,
    picks_ref,
    q_ref,
    pieces_ref,
    state_hbm,
    summary_hbm,
    out_ref,
    v_all,
    state_ref,
    summary_ref,
    sems,
):
    tiles = [pl.ds(n * STACK, STACK) for n in range(NX)]
    copies = []
    for n, tile in enumerate(tiles):
        copies.append(
            (
                pltpu.make_async_copy(state_hbm.at[tile, :], state_ref.at[tile, :], sems.at[0, n]),
                pltpu.make_async_copy(
                    summary_hbm.at[tile, :], summary_ref.at[tile, :], sems.at[1, n]
                ),
            )
        )
    for pair in copies:
        for copy in pair:
            copy.start()

    def arrive():
        for pair in copies:
            for copy in pair:
                copy.wait()

    def finish(n, acc):
        result = acc[:, :HD] / acc[:, HD : HD + 1] + summary_ref[tiles[n], :]
        result = result.astype(jnp.bfloat16)
        at = pl.multiple_of(((place_ref[3] + n) & (NX - 1)) * TILE, TILE)
        for g in range(QPK):
            out_ref[pl.ds(at, TILE), g * HD : (g + 1) * HD] = result[g * TILE : (g + 1) * TILE]

    @pl.when(place_ref[4] == 0)
    def _():
        arrive()
        for n in range(NX):
            finish(n, state_ref[tiles[n], :])

    @pl.when(place_ref[4] > 0)
    def _():
        chunks = [slice(n * BLOCK, (n + 1) * BLOCK) for n in range(PIECES * PART // BLOCK)]

        def scores(n):
            q = q_ref[tiles[n], :]
            return [contract(q, pieces_ref[chunk, :HD]) for chunk in chunks]

        far_values(place_ref, picks_ref, pieces_ref, v_all)
        arrive()
        after = scores(0)
        for n in range(NX):
            xs = after
            if n + 1 < NX:
                after = scores(n + 1)
            state = state_ref[tiles[n], :]
            top0 = state[:, 2 * HD - 1 :]
            top = jnp.maximum(top0, row_max(xs) * SCALE)
            acc = state * jnp.exp2(top0 - top)
            for chunk, x in zip(chunks, xs):
                w = jnp.exp2(x * SCALE - top).astype(jnp.bfloat16)
                acc += jnp.dot(w, v_all[chunk, :], preferred_element_type=jnp.float32)
            finish(n, acc)


def far_attention(place, picks, q, state, summary, pieces):
    whole = lambda *shape: pl.BlockSpec(shape, lambda i, place, picks: (0, 0))
    return pl.pallas_call(
        far_kernel,
        grid_spec=pltpu.PrefetchScalarGridSpec(
            num_scalar_prefetch=2,
            grid=(1,),
            in_specs=[whole(NX * STACK, HD), whole(PIECES * PART, 2 * HD), ANY, ANY],
            out_specs=whole(BLOCK, QPK * HD),
            scratch_shapes=[
                pltpu.VMEM((PIECES * PART, 2 * HD), jnp.bfloat16),
                pltpu.VMEM((NX * STACK, 2 * HD), jnp.float32),
                pltpu.VMEM((NX * STACK, HD), jnp.float32),
                pltpu.SemaphoreType.DMA((2, NX)),
            ],
        ),
        out_shape=jax.ShapeDtypeStruct((BLOCK, QPK * HD), jnp.bfloat16),
        compiler_params=params(60),
        cost_estimate=cost(1 << 20, MIB),
        name="far_attention",
    )(place, picks, q, pieces, state, summary)


def hold_kernel(after_ref, low_ref, high_ref, low_out, high_out):
    pass


def hold(after, low, high):
    return pl.pallas_call(
        hold_kernel,
        in_specs=[ANY] * 3,
        out_specs=[ANY] * 2,
        out_shape=[jax.ShapeDtypeStruct(low.shape, low.dtype)] * 2,
        input_output_aliases={1: 0, 2: 1},
        compiler_params=params(16),
        cost_estimate=cost(0, 0),
        name="hold",
    )(after, low, high)


def project_kernel(place_ref, att_ref, w0, *refs):
    out_ref = refs[-1]
    x, c = place_ref[3], place_ref[2]
    depth = QPK * HD

    def columns(by, start, width):
        at = ((x + by) & (NX - 1)) * depth + start
        return att_ref[:, pl.ds(pl.multiple_of(at, width), width)]

    acc = jnp.dot(columns(0, 0, depth), w0[...], preferred_element_type=jnp.float32)
    for core, (below, above, low, high) in ((c, refs[:4]), (1 - c, refs[4:8])):
        opposite = jnp.concatenate([low[...], high[...]], axis=0)
        for by, w in ((-1, below[...]), (1, above[...]), (2, opposite)):
            a = columns(by, core * WHALF, WHALF)
            acc += jnp.dot(a, w, preferred_element_type=jnp.float32)
    out_ref[...] = acc.astype(jnp.bfloat16)


def project(place, attended, w0, weights):
    width, tile = w0.shape[1], 1024
    return pl.pallas_call(
        project_kernel,
        grid_spec=pltpu.PrefetchScalarGridSpec(
            num_scalar_prefetch=1,
            grid=(width // tile,),
            in_specs=[pl.BlockSpec((TILE, NX * QPK * HD), lambda n, place: (0, 0))]
            + [pl.BlockSpec((w.shape[0], tile), lambda n, place: (0, n)) for w in (w0, *weights)],
            out_specs=pl.BlockSpec((TILE, tile), lambda n, place: (0, n)),
        ),
        out_shape=jax.ShapeDtypeStruct((TILE, width), jnp.bfloat16),
        compiler_params=params(),
        cost_estimate=cost(1 << 20, MIB),
        name="project",
    )(place, attended, w0, *weights)


def shift(x, axis, size, by):
    return lax.ppermute(x, axis, [(i, (i + by) % size) for i in range(size)])


def swap(x):
    return lax.ppermute(x, "c", [(0, 1), (1, 0)])


def to_plane(x):
    return lax.all_to_all(x, ("y", "c"), 0, 0, tiled=True)


def per_device(q, k, v, picks, w):
    z, y, c, x = (lax.axis_index(a).astype(jnp.int32) for a in ("z", "y", "c", "x"))
    place = jnp.stack([z, y, c, x, z * PIECES + y * NC + c])
    plane_picks = lax.dynamic_slice_in_dim(picks.reshape(picks.shape[0], -1), z * PIECES, PIECES, 0)

    half = lax.dynamic_slice_in_dim(w, c * WHALF, WHALF, 0)
    sides = [shift(half, "x", NX, 1), shift(half, "x", NX, -1)]

    kv, msg = pack(k, v)
    a, b = unpack(to_plane(msg))
    blocks = NZ * PIECES
    prev = lax.ppermute(kv, ("z", "y", "c"), [(i, i + 1) for i in range(blocks - 1)])

    up, down = [(a, b)], [(a, b)]
    for d in range(3):
        up.append(tuple(shift(h, "z", NZ, 1) for h in up[-1]))
        down.append(tuple(shift(h, "z", NZ, -1) for h in down[-1]))
    far = (shift(up[3][0], "z", NZ, 1), shift(down[3][1], "z", NZ, -1))
    rings = up + [far] + [down[3], down[2], down[1]]
    bufs = [h for pair in rings for h in pair]

    below, above, pieces, low, high = pick_pieces(place, plane_picks, bufs, prev, *sides)
    pieces = to_plane(pieces)
    low, high = shift(low, "x", NX, 1), shift(high, "x", NX, -1)
    stacked, state = near_attention(place, q, k, v, prev)
    summary = summary_attention(place, stacked, bufs)
    attended = far_attention(place, plane_picks, stacked, state, summary, pieces)
    low, high = hold(attended, low, high)

    rows = lax.all_to_all(attended.reshape(NX, TILE, QPK * HD), "x", 0, 0, tiled=True)
    rows = jnp.transpose(rows, (1, 0, 2)).reshape(TILE, NX * QPK * HD)
    weights = [below, above, low, high]
    return project(place, rows, w, weights + [swap(m) for m in weights])


def solution(mesh):
    fine = Mesh(mesh.devices.reshape(NZ, NY, NC, NX), ("z", "y", "c", "x"))
    ctx = ("z", "y", "c")
    in_specs = (P(ctx, "x"), P(ctx, "x"), P(ctx, "x"), P(None, "x", None), P("x", None))
    out_specs = P(("z", "y", "c", "x"), None)
    return jax.shard_map(
        per_device, mesh=fine, in_specs=in_specs, out_specs=out_specs, check_vma=False
    )
```

```python
import functools
import math

import jax
import jax.numpy as jnp
from jax import lax
from jax.experimental import pallas as pl
from jax.experimental.pallas import tpu as pltpu
from jax.sharding import Mesh
from jax.sharding import PartitionSpec as P

HD = 128
BLOCK = 512
QPK = 4
PICKS = 6
PIECES = 8
ROWS = BLOCK // PIECES
PART = PICKS * ROWS
MEAN_ROWS = 16
MSG = ROWS + MEAN_ROWS
HALF = PIECES // 2 * ROWS
NZ, NY, NC, NX = 8, 4, 2, 4
TILE = BLOCK // NX
STACK = TILE * QPK
SCALE = HD**-0.5 * math.log2(math.e)
WHALF = QPK * HD // NC
FAR = 1e30
MIB = 1 << 20

ANY = pl.BlockSpec(memory_space=pl.ANY)


def params(mib=40):
    return pltpu.CompilerParams(vmem_limit_bytes=mib * MIB)


def cost(flops, nbytes, trans=0):
    return pl.CostEstimate(flops=flops, bytes_accessed=nbytes, transcendentals=trans)


def pack_kernel(k_ref, v_ref, kv_ref, msg_ref):
    k = k_ref[...]
    v = v_ref[...]
    kv_ref[:, :HD] = k
    kv_ref[:, HD:] = v
    mk = jnp.sum(k.astype(jnp.float32), axis=0, keepdims=True) * (1.0 / BLOCK)
    mv = jnp.sum(v.astype(jnp.float32), axis=0, keepdims=True) * (1.0 / BLOCK)
    mean = jnp.concatenate([mk, mv], axis=1).astype(jnp.bfloat16)
    mean = jnp.broadcast_to(mean, (MEAN_ROWS, 2 * HD))
    for r in range(PIECES):
        rows = slice(r * ROWS, (r + 1) * ROWS)
        msg_ref[r, :ROWS, :HD] = k_ref[rows, :]
        msg_ref[r, :ROWS, HD:] = v_ref[rows, :]
        msg_ref[r, ROWS:, :] = mean


def pack(k, v):
    return pl.pallas_call(
        pack_kernel,
        out_shape=[
            jax.ShapeDtypeStruct((BLOCK, 2 * HD), jnp.bfloat16),
            jax.ShapeDtypeStruct((PIECES, MSG, 2 * HD), jnp.bfloat16),
        ],
        compiler_params=params(16),
        cost_estimate=cost(1 << 18, MIB),
        name="pack",
    )(k, v)


def unpack_kernel(msg_ref, a_ref, b_ref):
    row = lax.broadcasted_iota(jnp.int32, (MEAN_ROWS, 2 * HD), 0)
    for h, out in enumerate((a_ref, b_ref)):
        means = jnp.zeros((MEAN_ROWS, 2 * HD), jnp.float32)
        for i in range(PIECES // 2):
            s = h * (PIECES // 2) + i
            out[i * ROWS : (i + 1) * ROWS, :] = msg_ref[s, :ROWS, :]
            means = jnp.where(row == i, msg_ref[s, ROWS:, :].astype(jnp.float32), means)
        out[HALF:, :] = means.astype(jnp.bfloat16)


def unpack(msg):
    return pl.pallas_call(
        unpack_kernel,
        out_shape=[jax.ShapeDtypeStruct((HALF + MEAN_ROWS, 2 * HD), jnp.bfloat16)] * 2,
        compiler_params=params(16),
        cost_estimate=cost(1 << 18, MIB),
        name="unpack",
    )(msg)


def choose(refs, index, act):
    if len(refs) == 1:
        act(refs[0])
        return
    half = len(refs) // 2
    lax.cond(
        index < half,
        lambda: choose(refs[:half], index, act),
        lambda: choose(refs[half:], index - half, act),
    )


def pick_kernel(place_ref, picks_ref, *refs):
    bufs, below, above = refs[: 2 * NZ], refs[2 * NZ + 1], refs[2 * NZ + 2]
    out, low, high, sem, side_sem = refs[-5:]
    rows = WHALF // 2
    sides = [
        pltpu.make_async_copy(below.at[:rows, :], low, side_sem.at[0]),
        pltpu.make_async_copy(above.at[rows:, :], high, side_sem.at[1]),
    ]

    def step(n, carry):
        p = picks_ref[lax.div(n, PICKS), 1 + lax.rem(n, PICKS)]
        d = (place_ref[0] - lax.shift_right_logical(p, 3)) & (NZ - 1)
        h = lax.shift_right_logical(p, 2) & 1
        start = pl.multiple_of((p & 3) * ROWS, ROWS)
        to = pl.multiple_of(n * ROWS, ROWS)

        def act(buf):
            pltpu.make_async_copy(
                buf.at[pl.ds(start, ROWS), :], out.at[pl.ds(to, ROWS), :], sem
            ).start()

        choose(bufs, d * 2 + h, act)
        return carry

    for copy in sides:
        copy.start()
    lax.fori_loop(0, PIECES * PICKS, step, 0, unroll=8)
    pltpu.make_async_copy(out, out, sem).wait()
    for copy in sides:
        copy.wait()


def pick_pieces(place, picks, bufs, prev, below, above):
    half = jax.ShapeDtypeStruct((WHALF // 2, below.shape[1]), jnp.bfloat16)
    whole = lambda s: pl.BlockSpec(s.shape, lambda i, place, picks: (0, 0))
    pieces = jax.ShapeDtypeStruct((PIECES * PART, 2 * HD), jnp.bfloat16)
    side = jax.ShapeDtypeStruct(below.shape, below.dtype)
    return pl.pallas_call(
        pick_kernel,
        grid_spec=pltpu.PrefetchScalarGridSpec(
            num_scalar_prefetch=2,
            grid=(1,),
            in_specs=[ANY] * (2 * NZ + 3),
            out_specs=[ANY, ANY, whole(pieces), whole(half), whole(half)],
            scratch_shapes=[pltpu.SemaphoreType.DMA(()), pltpu.SemaphoreType.DMA((2,))],
        ),
        out_shape=[side, side, pieces, half, half],
        input_output_aliases={3 + 2 * NZ: 0, 4 + 2 * NZ: 1},
        compiler_params=params(60),
        cost_estimate=cost(0, MIB),
        name="pick_pieces",
    )(place, picks, *bufs, prev, below, above)


def contract(a, b):
    return lax.dot_general(a, b, (((1,), (1,)), ((), ())), preferred_element_type=jnp.float32)


def row_max(xs):
    top = jnp.max(xs[0], axis=1, keepdims=True)
    for x in xs[1:]:
        top = jnp.maximum(top, jnp.max(x, axis=1, keepdims=True))
    return top


def save_state(out_ref, rows, acc, top):
    lane = lax.broadcasted_iota(jnp.int32, (STACK, HD), 1)
    out_ref[rows, :HD] = acc[:, :HD]
    out_ref[rows, HD:] = jnp.where(lane < HD // 2, acc[:, HD:], top)


def near_kernel(place_ref, q_ref, k_ref, v_ref, prev_ref, stacked_ref, out_ref, own_v, prev_v):
    ones = jnp.ones((BLOCK, HD), jnp.bfloat16)
    own_v[:, :HD] = v_ref[...]
    own_v[:, HD:] = ones
    prev_v[:, :HD] = prev_ref[:, HD:]
    prev_v[:, HD:] = ones
    key = lax.broadcasted_iota(jnp.int32, (STACK, BLOCK), 1)
    token = lax.rem(lax.broadcasted_iota(jnp.int32, (STACK, BLOCK), 0), TILE)
    pen = jnp.where(place_ref[4] == 0, FAR, 0.0)

    def scores(i):
        at = pl.multiple_of(((place_ref[3] + i) & (NX - 1)) * TILE, TILE)
        for g in range(QPK):
            rows = slice(i * STACK + g * TILE, i * STACK + (g + 1) * TILE)
            stacked_ref[rows, :] = q_ref[pl.ds(at, TILE), g * HD : (g + 1) * HD]
        q = stacked_ref[i * STACK : (i + 1) * STACK, :]
        own = jnp.where(key - token <= at, contract(q, k_ref[...]) * SCALE, -FAR)
        return own, contract(q, prev_ref[:, :HD]) * SCALE

    after = scores(0)
    for i in range(NX):
        own, prev = after
        if i + 1 < NX:
            after = scores(i + 1)
        top = jnp.maximum(row_max([own]), row_max([prev]) - pen)
        own = jnp.exp2(own - top).astype(jnp.bfloat16)
        prev = jnp.exp2(prev - (top + pen)).astype(jnp.bfloat16)
        acc = jnp.dot(own, own_v[...], preferred_element_type=jnp.float32)
        acc += jnp.dot(prev, prev_v[...], preferred_element_type=jnp.float32)
        save_state(out_ref, slice(i * STACK, (i + 1) * STACK), acc, top)


def near_attention(place, q, k, v, prev):
    whole = lambda *shape: pl.BlockSpec(shape, lambda i, place: (0, 0))
    return pl.pallas_call(
        near_kernel,
        grid_spec=pltpu.PrefetchScalarGridSpec(
            num_scalar_prefetch=1,
            grid=(1,),
            in_specs=[
                whole(BLOCK, QPK * HD),
                whole(BLOCK, HD),
                whole(BLOCK, HD),
                whole(BLOCK, 2 * HD),
            ],
            out_specs=[whole(NX * STACK, HD), whole(NX * STACK, 2 * HD)],
            scratch_shapes=[pltpu.VMEM((BLOCK, 2 * HD), jnp.bfloat16)] * 2,
        ),
        out_shape=[
            jax.ShapeDtypeStruct((NX * STACK, HD), jnp.bfloat16),
            jax.ShapeDtypeStruct((NX * STACK, 2 * HD), jnp.float32),
        ],
        compiler_params=params(),
        cost_estimate=cost(1 << 20, MIB),
        name="near_attention",
    )(place, q, k, v, prev)


def summary_kernel(place_ref, q_ref, *refs):
    means, (out_ref, mean_k, mean_v) = refs[: 2 * NZ], refs[2 * NZ :]
    z, block = place_ref[0], place_ref[4]
    for s, mean in enumerate(means):
        rows = slice(s * MEAN_ROWS, (s + 1) * MEAN_ROWS)
        mean_k[rows, :] = mean[:, :HD]
        mean_v[rows, :HD] = mean[:, HD:]
    mean_v[:, HD:] = jnp.ones((2 * NZ * MEAN_ROWS, HD), jnp.bfloat16)

    s = lax.broadcasted_iota(jnp.int32, (1, 2 * NZ * MEAN_ROWS), 1)
    i4 = s & (MEAN_ROWS - 1)
    half = lax.shift_right_logical(s, 4) & 1
    zs = (z - lax.shift_right_logical(s, 5)) & (NZ - 1)
    number = zs * PIECES + half * (PIECES // 2) + i4
    bias = jnp.where((i4 < PIECES // 2) & (number < block), 0.0, -FAR)

    def scores(i):
        return contract(q_ref[i * STACK : (i + 1) * STACK, :], mean_k[...]) * SCALE + bias

    after = scores(0)
    for i in range(NX):
        sums = after
        if i + 1 < NX:
            after = scores(i + 1)
        top = jnp.maximum(row_max([sums]), 0.0)
        w = jnp.exp2(sums - top).astype(jnp.bfloat16)
        summary = jnp.dot(w, mean_v[...], preferred_element_type=jnp.float32)
        total = summary[:, HD:] + jnp.exp2(-top)
        out_ref[i * STACK : (i + 1) * STACK, :] = summary[:, :HD] / total


def summary_attention(place, q, bufs):
    whole = lambda rows, columns, at: pl.BlockSpec((rows, columns), lambda i, place: (at, 0))
    mean_count = 2 * NZ * MEAN_ROWS
    return pl.pallas_call(
        summary_kernel,
        grid_spec=pltpu.PrefetchScalarGridSpec(
            num_scalar_prefetch=1,
            grid=(1,),
            in_specs=[whole(NX * STACK, HD, 0)]
            + [whole(MEAN_ROWS, 2 * HD, HALF // MEAN_ROWS)] * (2 * NZ),
            out_specs=whole(NX * STACK, HD, 0),
            scratch_shapes=[
                pltpu.VMEM((mean_count, HD), jnp.bfloat16),
                pltpu.VMEM((mean_count, 2 * HD), jnp.bfloat16),
            ],
        ),
        out_shape=jax.ShapeDtypeStruct((NX * STACK, HD), jnp.float32),
        compiler_params=params(60),
        cost_estimate=cost(1 << 20, MIB),
        name="summary_attention",
    )(place, q, *bufs)


def far_values(place_ref, picks_ref, pieces_ref, v_all):
    block = place_ref[4]
    own = block & (PIECES - 1)
    for j in range(PICKS):
        p = picks_ref[own, j + 1]
        bad = p == block
        for e in range(j + 1):
            bad = bad | (p == picks_ref[own, e])
        keep = jnp.where(bad, 0.0, 1.0)
        ones = jnp.full((ROWS, HD), keep, jnp.float32).astype(jnp.bfloat16)
        for s in range(PIECES):
            at = slice(s * PART + j * ROWS, s * PART + (j + 1) * ROWS)
            v_all[at, :HD] = (pieces_ref[at, HD:].astype(jnp.float32) * keep).astype(jnp.bfloat16)
            v_all[at, HD:] = ones


def far_kernel(
    place_ref,
    picks_ref,
    q_ref,
    pieces_ref,
    state_hbm,
    summary_hbm,
    out_ref,
    v_all,
    state_ref,
    summary_ref,
    sems,
):
    tiles = [pl.ds(n * STACK, STACK) for n in range(NX)]
    copies = []
    for n, tile in enumerate(tiles):
        copies.append(
            (
                pltpu.make_async_copy(state_hbm.at[tile, :], state_ref.at[tile, :], sems.at[0, n]),
                pltpu.make_async_copy(
                    summary_hbm.at[tile, :], summary_ref.at[tile, :], sems.at[1, n]
                ),
            )
        )
    for pair in copies:
        for copy in pair:
            copy.start()

    def arrive():
        for pair in copies:
            for copy in pair:
                copy.wait()

    def finish(n, acc):
        result = acc[:, :HD] / acc[:, HD : HD + 1] + summary_ref[tiles[n], :]
        result = result.astype(jnp.bfloat16)
        at = pl.multiple_of(((place_ref[3] + n) & (NX - 1)) * TILE, TILE)
        for g in range(QPK):
            out_ref[pl.ds(at, TILE), g * HD : (g + 1) * HD] = result[g * TILE : (g + 1) * TILE]

    @pl.when(place_ref[4] == 0)
    def _():
        arrive()
        for n in range(NX):
            finish(n, state_ref[tiles[n], :])

    @pl.when(place_ref[4] > 0)
    def _():
        chunks = [slice(n * BLOCK, (n + 1) * BLOCK) for n in range(PIECES * PART // BLOCK)]

        def scores(n):
            q = q_ref[tiles[n], :]
            return [contract(q, pieces_ref[chunk, :HD]) for chunk in chunks]

        far_values(place_ref, picks_ref, pieces_ref, v_all)
        arrive()
        after = scores(0)
        for n in range(NX):
            xs = after
            if n + 1 < NX:
                after = scores(n + 1)
            state = state_ref[tiles[n], :]
            top0 = state[:, 2 * HD - 1 :]
            top = jnp.maximum(top0, row_max(xs) * SCALE)
            acc = state * jnp.exp2(top0 - top)
            for chunk, x in zip(chunks, xs):
                w = jnp.exp2(x * SCALE - top).astype(jnp.bfloat16)
                acc += jnp.dot(w, v_all[chunk, :], preferred_element_type=jnp.float32)
            finish(n, acc)


def far_attention(place, picks, q, state, summary, pieces):
    whole = lambda *shape: pl.BlockSpec(shape, lambda i, place, picks: (0, 0))
    return pl.pallas_call(
        far_kernel,
        grid_spec=pltpu.PrefetchScalarGridSpec(
            num_scalar_prefetch=2,
            grid=(1,),
            in_specs=[whole(NX * STACK, HD), whole(PIECES * PART, 2 * HD), ANY, ANY],
            out_specs=whole(BLOCK, QPK * HD),
            scratch_shapes=[
                pltpu.VMEM((PIECES * PART, 2 * HD), jnp.bfloat16),
                pltpu.VMEM((NX * STACK, 2 * HD), jnp.float32),
                pltpu.VMEM((NX * STACK, HD), jnp.float32),
                pltpu.SemaphoreType.DMA((2, NX)),
            ],
        ),
        out_shape=jax.ShapeDtypeStruct((BLOCK, QPK * HD), jnp.bfloat16),
        compiler_params=params(60),
        cost_estimate=cost(1 << 20, MIB),
        name="far_attention",
    )(place, picks, q, pieces, state, summary)


def hold_kernel(after_ref, low_ref, high_ref, low_out, high_out):
    pass


def hold(after, low, high):
    return pl.pallas_call(
        hold_kernel,
        in_specs=[ANY] * 3,
        out_specs=[ANY] * 2,
        out_shape=[jax.ShapeDtypeStruct(low.shape, low.dtype)] * 2,
        input_output_aliases={1: 0, 2: 1},
        compiler_params=params(16),
        cost_estimate=cost(0, 0),
        name="hold",
    )(after, low, high)


def project_kernel(place_ref, att_ref, w0, *refs):
    out_ref = refs[-1]
    x, c = place_ref[3], place_ref[2]
    depth = QPK * HD

    def columns(by, start, width):
        at = ((x + by) & (NX - 1)) * depth + start
        return att_ref[:, pl.ds(pl.multiple_of(at, width), width)]

    acc = jnp.dot(columns(0, 0, depth), w0[...], preferred_element_type=jnp.float32)
    for core, (below, above, low, high) in ((c, refs[:4]), (1 - c, refs[4:8])):
        opposite = jnp.concatenate([low[...], high[...]], axis=0)
        for by, w in ((-1, below[...]), (1, above[...]), (2, opposite)):
            a = columns(by, core * WHALF, WHALF)
            acc += jnp.dot(a, w, preferred_element_type=jnp.float32)
    out_ref[...] = acc.astype(jnp.bfloat16)


def project(place, attended, w0, weights):
    width, tile = w0.shape[1], 1024
    return pl.pallas_call(
        project_kernel,
        grid_spec=pltpu.PrefetchScalarGridSpec(
            num_scalar_prefetch=1,
            grid=(width // tile,),
            in_specs=[pl.BlockSpec((TILE, NX * QPK * HD), lambda n, place: (0, 0))]
            + [pl.BlockSpec((w.shape[0], tile), lambda n, place: (0, n)) for w in (w0, *weights)],
            out_specs=pl.BlockSpec((TILE, tile), lambda n, place: (0, n)),
        ),
        out_shape=jax.ShapeDtypeStruct((TILE, width), jnp.bfloat16),
        compiler_params=params(),
        cost_estimate=cost(1 << 20, MIB),
        name="project",
    )(place, attended, w0, *weights)


def shift(x, axis, size, by):
    return lax.ppermute(x, axis, [(i, (i + by) % size) for i in range(size)])


def swap(x):
    return lax.ppermute(x, "c", [(0, 1), (1, 0)])


def to_plane(x):
    return lax.all_to_all(x, ("y", "c"), 0, 0, tiled=True)


def per_device(q, k, v, picks, w):
    z, y, c, x = (lax.axis_index(a).astype(jnp.int32) for a in ("z", "y", "c", "x"))
    place = jnp.stack([z, y, c, x, z * PIECES + y * NC + c])
    plane_picks = lax.dynamic_slice_in_dim(picks.reshape(picks.shape[0], -1), z * PIECES, PIECES, 0)

    half = lax.dynamic_slice_in_dim(w, c * WHALF, WHALF, 0)
    sides = [shift(half, "x", NX, 1), shift(half, "x", NX, -1)]

    kv, msg = pack(k, v)
    a, b = unpack(to_plane(msg))
    blocks = NZ * PIECES
    prev = lax.ppermute(kv, ("z", "y", "c"), [(i, i + 1) for i in range(blocks - 1)])

    up, down = [(a, b)], [(a, b)]
    for d in range(3):
        up.append(tuple(shift(h, "z", NZ, 1) for h in up[-1]))
        down.append(tuple(shift(h, "z", NZ, -1) for h in down[-1]))
    far = (shift(up[3][0], "z", NZ, 1), shift(down[3][1], "z", NZ, -1))
    rings = up + [far] + [down[3], down[2], down[1]]
    bufs = [h for pair in rings for h in pair]

    below, above, pieces, low, high = pick_pieces(place, plane_picks, bufs, prev, *sides)
    pieces = to_plane(pieces)
    low, high = shift(low, "x", NX, 1), shift(high, "x", NX, -1)
    stacked, state = near_attention(place, q, k, v, prev)
    summary = summary_attention(place, stacked, bufs)
    attended = far_attention(place, plane_picks, stacked, state, summary, pieces)
    low, high = hold(attended, low, high)

    rows = lax.all_to_all(attended.reshape(NX, TILE, QPK * HD), "x", 0, 0, tiled=True)
    rows = jnp.transpose(rows, (1, 0, 2)).reshape(TILE, NX * QPK * HD)
    weights = [below, above, low, high]
    return project(place, rows, w, weights + [swap(m) for m in weights])


def solution(mesh):
    fine = Mesh(mesh.devices.reshape(NZ, NY, NC, NX), ("z", "y", "c", "x"))
    ctx = ("z", "y", "c")
    in_specs = (P(ctx, "x"), P(ctx, "x"), P(ctx, "x"), P(None, "x", None), P("x", None))
    out_specs = P(("z", "y", "c", "x"), None)
    return jax.shard_map(
        per_device, mesh=fine, in_specs=in_specs, out_specs=out_specs, check_vma=False
    )
```
